512 devices in a mesh: wide: 64 (over y, x, core), narrow: 8 (over z).
Axes of the slice: x: 4, y: 8, z: 8, core: 2. Of those that a mesh axis runs over, the one named last changes fastest.
Arguments:
- base: float32 [2, 192, 192, 192], P(None, 'wide', 'narrow'), may hold values from -6 to 6
- fine_psi: float32 [2048, 2, 16, 256], P(('wide', 'narrow')), may hold values from -6 to 6
- counts: int32 [512], P(('wide', 'narrow')), may hold values from 1 to 4, as said below
- neighbors: int32 [2048, 6], P(('wide', 'narrow')), may hold values from -1 to 2047, as said below
- base_cell: int32 [2048, 6, 3], replicated, may hold values from 0 to 191, as said below
Outputs:
- drifted: float32 [2, 192, 192, 192], P(None, 'wide', 'narrow')
- fine_out: float32 [2048, 2, 16, 256], P(('wide', 'narrow'))
The draws below stay inside these ranges and needn't reach their ends.
Inputs may be any that keep to these rules, and one draw needn't show every extreme that they name: Each device's live slots are its first counts entries. `neighbors`: A present neighbour is a live slot (device * 4 + slot) of the same device or of the device just before or after it in the order of wide+narrow, wrapping around; faces 2k and 2k + 1 are the lower and upper faces along grid dimension k; padded slots hold -1 everywhere. `base_cell`: the base cell just outside the centre of each face of the group.
All inputs are finite; a program needn't handle non-finite values.
Results may differ from the reference program's by a relative error of at most 0.00024.
Values sent between devices are 32-bit elements; how exact they have to be, the bound alone decides.
No kernel may reach another device: no remote copies, remote signals or barrier semaphores. Data moves between devices by JAX's collectives and lax.ppermute only.
A program may use at most 64 MiB of HBM per device.

```python
import jax
import jax.numpy as jnp
import numpy as np
from jax import lax

NB = 192
GROUP_EDGE = 16
CAP = 4
SUBCYCLES = 2
GROUPS = 2048
N_WIDE = 64
N_NARROW = 8


def make_counts(key):
    devices_all = N_WIDE * N_NARROW
    folded = jax.random.fold_in(key, 11)
    first_key, second_key, third_key = jax.random.split(folded, 3)
    modest = 1 + jax.random.randint(first_key, (devices_all,), 0, max(CAP // 2, 1))
    heavy = jax.random.randint(second_key, (devices_all,), 0, 8) == 0
    chosen = jax.random.randint(third_key, (), 0, devices_all)
    result = jnp.where(heavy, CAP, modest)
    result = jnp.where(jnp.arange(devices_all) == chosen, CAP, result)
    result = jnp.where(jnp.arange(devices_all) == devices_all - 1, CAP, result)
    return result.astype(jnp.int32)


def draw_counts(key, part):
    return make_counts(key)


def draw_neighbors(key, part):
    devices_all = N_WIDE * N_NARROW
    slot_total = devices_all * CAP
    counts_all = make_counts(key)
    folded = jax.random.fold_in(key, 23)
    first_key, second_key, third_key = jax.random.split(folded, 3)
    slot_ids = jnp.arange(slot_total, dtype=jnp.int32)
    home = slot_ids // CAP
    local_slot = slot_ids - home * CAP
    stepping = jax.random.randint(first_key, (slot_total, 6), -1, 2)
    owner_device = (home[:, None] + stepping + devices_all) % devices_all
    raw_pick = jax.random.randint(second_key, (slot_total, 6), 0, 1 << 20)
    target = raw_pick % counts_all[owner_device]
    present = jax.random.randint(third_key, (slot_total, 6), 0, 4) > 0
    live = local_slot < counts_all[home]
    global_ids = owner_device * CAP + target
    result = jnp.where(present & live[:, None], global_ids, -1).astype(jnp.int32)
    result = result.at[0, 0].set(slot_total - 1)
    result = result.at[0, 1].set(CAP)
    result = result.at[0, 3].set(CAP)
    result = result.at[0, 5].set(CAP)
    return result.astype(jnp.int32)


def draw_base_cell(key, part):
    slot_total = N_WIDE * N_NARROW * CAP
    folded = jax.random.fold_in(key, 37)
    anchors = jax.random.randint(folded, (slot_total, 3), 0, NB // 8) * 8
    offsets = np.full((6, 3), 4, dtype=np.int32)
    for face_index in range(6):
        offsets[face_index, face_index // 2] = -1 if face_index % 2 == 0 else 8
    cells = (anchors[:, None, :] + jnp.asarray(offsets)[None, :, :] + NB) % NB
    return cells.astype(jnp.int32)


def shard_levels(rng, shape, shards, least, top_value):
    loudness = 1.0
    for axis_at, shards_of in shards:
        steps = jax.random.uniform(jax.random.fold_in(jax.random.fold_in(rng, 6), axis_at), (shards_of,), jnp.float32, least / len(shards), top_value / len(shards))
        loudness = loudness * jnp.repeat(jnp.exp(steps), shape[axis_at] // shards_of).reshape((-1,) + (1,) * (len(shape) - 1 - axis_at))
    return loudness


def gaussian(rng, dims, scale, bound, pieces=(), kind=jnp.bfloat16):
    factor_of = shard_levels(rng, dims, pieces, -0.22, 0.18) if pieces else 1.0
    values = jax.random.normal(rng, dims, jnp.float32) * scale * factor_of
    return jnp.minimum(jnp.maximum(values, -bound), bound).astype(kind)


def setup_inputs(seed: int = 0) -> dict:
    streams_of = jax.random.split(jax.random.key(seed), 6)
    return {
        "base": gaussian(streams_of[0], (2, NB, NB, NB), 1.0, 6.0, ((1, 64), (2, 8)), jnp.float32),
        "fine_psi": gaussian(streams_of[1], (GROUPS, 2, GROUP_EDGE, GROUP_EDGE * GROUP_EDGE), 1.0, 6.0, ((0, 512),), jnp.float32),
        "counts": draw_counts(jax.random.fold_in(streams_of[5], 71), 0),
        "neighbors": draw_neighbors(jax.random.fold_in(streams_of[5], 71), 0),
        "base_cell": draw_base_cell(jax.random.fold_in(streams_of[5], 71), 0),
    }


PHASE_RATE = 8.0
TAYLOR_STEP = 0.6


def taylor_matrix():
    position = jnp.arange(24)
    offset = position[:, None] - position[None, :]
    laplace = jnp.where(offset == 0, -2.0, 0.0) + jnp.where(jnp.abs(offset) == 1, 1.0, 0.0)
    laplace = laplace.astype(jnp.float32)
    squared = jnp.dot(laplace, laplace, precision=lax.Precision.HIGHEST)
    cubed = jnp.dot(squared, laplace, precision=lax.Precision.HIGHEST)
    fourth = jnp.dot(squared, squared, precision=lax.Precision.HIGHEST)
    identity = jnp.eye(24, dtype=jnp.float32)
    real_full = identity - (TAYLOR_STEP ** 2 / 2.0) * squared + (TAYLOR_STEP ** 4 / 24.0) * fourth
    imag_full = TAYLOR_STEP * laplace - (TAYLOR_STEP ** 3 / 6.0) * cubed
    real_rows = real_full[4:20]
    imag_rows = imag_full[4:20]
    return jnp.concatenate([jnp.concatenate([real_rows, -imag_rows], 1), jnp.concatenate([imag_rows, real_rows], 1)], 0)


def drift_base(base):
    grid_len = base.shape[1]
    frequency = jnp.arange(grid_len)
    signed_freq = jnp.where(frequency < grid_len // 2, frequency, frequency - grid_len)
    wavenumber = (2.0 * jnp.pi / grid_len) * signed_freq.astype(base.dtype)
    rotation = PHASE_RATE * wavenumber * wavenumber
    factor = lax.complex(jnp.cos(rotation), -jnp.sin(rotation))
    spectrum = jnp.fft.fftn(lax.complex(base[0], base[1]))
    spectrum = spectrum * factor[:, None, None]
    spectrum = spectrum * factor[None, :, None]
    spectrum = spectrum * factor[None, None, :]
    result = jnp.fft.ifftn(spectrum)
    return jnp.stack([jnp.real(result), jnp.imag(result)]).astype(base.dtype)


def ghost_layers(face_all, neighbor_ids, edge_pairs):
    clipped = jnp.maximum(neighbor_ids, 0)
    taken = jnp.take(face_all, clipped, axis=0)
    constant = jnp.broadcast_to(edge_pairs[:, :, None, None], taken.shape)
    return jnp.where((neighbor_ids >= 0)[:, None, None, None], taken, constant)


def advance_sweep(patches, lower_ghost, upper_ghost, matrix):
    slot_total = patches.shape[0]
    extended = jnp.concatenate([lower_ghost, patches, upper_ghost], axis=2)
    flattened = extended.reshape(slot_total, 48, -1)
    updated = jnp.einsum('kj,gjn->gkn', matrix, flattened, precision=lax.Precision.HIGHEST)
    updated = updated.reshape(slot_total, 2, 16, 16, 16)
    return jnp.transpose(updated, (0, 1, 3, 4, 2)).reshape(slot_total, 2, 16, 256)


def reference(base, fine_psi, counts, neighbors, base_cell):
    drifted = drift_base(base)
    picked = drifted[:, base_cell[:, :, 0], base_cell[:, :, 1], base_cell[:, :, 2]]
    edge_values = jnp.transpose(picked, (1, 2, 0))
    matrix = taylor_matrix()
    patches = fine_psi
    for subcycle in range(SUBCYCLES):
        for sweep_dim in range(3):
            lower_ghost = ghost_layers(patches[:, :, 12:, :], neighbors[:, 2 * sweep_dim], edge_values[:, 2 * sweep_dim])
            upper_ghost = ghost_layers(patches[:, :, :4, :], neighbors[:, 2 * sweep_dim + 1], edge_values[:, 2 * sweep_dim + 1])
            patches = advance_sweep(patches, lower_ghost, upper_ghost, matrix)
    slot_ids = jnp.arange(patches.shape[0], dtype=jnp.int32)
    owners = slot_ids // CAP
    live = (slot_ids - owners * CAP) < counts[owners]
    fine_out = jnp.where(live[:, None, None, None], patches, jnp.zeros_like(patches))
    return drifted, fine_out
```

```python
import jax
import jax.numpy as jnp
import ml_dtypes
import numpy as np
from jax import lax
from jax.experimental import pallas as pl
from jax.experimental.pallas import tpu as pltpu
from jax.sharding import PartitionSpec as P

SUBCYCLES = 2
PHASE_RATE = 8.0
TAYLOR_STEP = 0.6
EDGE = 16
CELLS = EDGE * EDGE
LANES = 128
REACH = 6
VMEM = pl.BlockSpec(memory_space=pltpu.VMEM)
SMEM = pl.BlockSpec(memory_space=pltpu.SMEM)
PARAMS = pltpu.CompilerParams(vmem_limit_bytes=48 * 2**20)
F32 = jnp.float32
BF16 = jnp.bfloat16


def two_parts(matrix):
    high = matrix.astype(ml_dtypes.bfloat16)
    low = (matrix - high.astype(np.float64)).astype(ml_dtypes.bfloat16)
    return high, low


def circulant(length):
    signed = np.fft.fftfreq(length, 1.0 / length)
    phase = np.exp(-1j * PHASE_RATE * (2.0 * np.pi * signed / length) ** 2)
    kernel = np.fft.ifft(phase)
    index = np.arange(length)
    matrix = kernel[(index[:, None] - index[None, :]) % length]
    return matrix.real, matrix.imag


def taylor_parts():
    laplace = -2.0 * np.eye(24) + np.eye(24, k=1) + np.eye(24, k=-1)
    squared = laplace @ laplace
    c = TAYLOR_STEP
    real = np.eye(24) - c**2 / 2.0 * squared + c**4 / 24.0 * squared @ squared
    imag = c * laplace - c**3 / 6.0 * squared @ laplace
    parts = []
    for rows in (real[4:20], imag[4:20]):
        ghost = np.zeros((EDGE, EDGE))
        ghost[:, 12:] = rows[:, :4]
        ghost[:, :4] = rows[:, 20:]
        parts.append((rows[:, 4:20], ghost))
    return parts


def sweep_tables():
    (own_r, ghost_r), (own_i, ghost_i) = taylor_parts()
    left = np.concatenate(
        [
            np.block([[own_r, -own_i], [own_i, own_r]]),
            np.block([[ghost_r, -ghost_i], [ghost_i, ghost_r]]),
        ],
        1,
    )
    eye = np.eye(EDGE)

    def right(form):
        return np.block([[form(own_r), form(own_i)], [form(ghost_r), form(ghost_i)]])

    middle = right(lambda t: np.kron(t.T, eye))
    last = right(lambda t: np.kron(eye, t.T))
    high, low = two_parts(left)
    return np.concatenate([high, high, low], 1), *two_parts(middle), *two_parts(last)


def split(values):
    high = values.astype(BF16)
    return high, (values - high.astype(F32)).astype(BF16)


def mm(a, b):
    return jnp.dot(a, b, preferred_element_type=F32)


def mm3(a, b):
    return mm(a[0], b[0]) + (mm(a[1], b[0]) + mm(a[0], b[1]))


def along_last(rows_here, cols_here, parts, base_ref, rh, rl, ih, il, out_ref):
    plane = rows_here * cols_here
    x = split(base_ref[...])
    pr = mm3(x, (rh[...], rl[...]))
    pi = mm3(x, (ih[...], il[...]))
    done = (pr[:plane] - pi[plane:], pi[:plane] + pr[plane:])
    chunk = done[0].shape[1] // parts
    pad = jnp.zeros((cols_here, LANES - rows_here * chunk), F32)
    for n in range(parts):
        for p in range(2):
            pieces = [
                done[p][cols_here * x : cols_here * (x + 1), chunk * n : chunk * (n + 1)]
                for x in range(rows_here)
            ]
            row = (2 * n + p) * cols_here
            out_ref[row : row + cols_here, :] = jnp.concatenate(pieces + [pad], 1)


def along_second(rows_here, chunk, wide, x_ref, wh, wl, out_ref):
    done = mm3((wh[...], wl[...]), split(x_ref[...]))
    pad = jnp.zeros((wide, LANES - rows_here * chunk), F32)
    for p in range(2):
        for x in range(rows_here):
            pieces = [
                done[(p * rows_here + j) * wide : (p * rows_here + j + 1) * wide, chunk * x : chunk * (x + 1)]
                for j in range(rows_here)
            ]
            out_ref[pl.ds(p * rows_here + x, wide, stride=8), :] = jnp.concatenate(pieces + [pad], 1)
    blank = jnp.zeros((wide, LANES), F32)
    for r in range(2 * rows_here, 8):
        out_ref[pl.ds(r, wide, stride=8), :] = blank


def along_first(rows_here, chunk, wide, narrow, slots, place_ref, cell_ref, x_ref, wh, wl, out_ref, o_ref, v_ref):
    used = rows_here * chunk
    lines = rows_here * wide
    groups = cell_ref.shape[1]
    o_ref[...] = mm3((wh[...], wl[...]), split(x_ref[...]))
    turned = []
    for p in range(2):
        natural = [o_ref[pl.ds(p * rows_here + x, wide, stride=8), :] for x in range(rows_here)]
        natural.append(jnp.zeros((256 - lines, LANES), F32))
        turned.append(jnp.concatenate(natural, 0).T[:used])
    high, low = split(jnp.concatenate(turned, 0))
    left = jnp.concatenate([high, low], 0)
    second_start = place_ref[0] * rows_here
    last_start = place_ref[1] * chunk
    step = 256
    line_of = lax.broadcasted_iota(jnp.int32, (256, step), 0)
    lane_of = lax.broadcasted_iota(jnp.int32, (used, step), 0)

    def body(c, carry):
        at = pl.multiple_of(c * step, step)
        for f in range(6):
            first = cell_ref[f : f + 1, pl.ds(at, step)]
            second = cell_ref[6 + f : 7 + f, pl.ds(at, step)] - second_start
            last = cell_ref[12 + f : 13 + f, pl.ds(at, step)] - last_start
            mine = (second >= 0) & (second < rows_here) & (last >= 0) & (last < chunk)
            owner = first // rows_here
            line = (first - owner * rows_here) * wide + owner
            lane = jnp.where(mine, second * chunk + last, -1)
            hot = jnp.where(line_of == line, 1.0, 0.0).astype(BF16)
            taken = mm(left, hot)
            keep = lane_of == lane
            for p in range(2):
                both = taken[p * used : (p + 1) * used] + taken[(2 + p) * used : (3 + p) * used]
                v_ref[p * 8 + f : p * 8 + f + 1, pl.ds(at + LANES, step)] = jnp.sum(
                    jnp.where(keep, both, 0.0), axis=0, keepdims=True
                )
        return carry

    lax.fori_loop(0, groups // step, body, 0)
    v_ref[:, :LANES] = v_ref[:, groups : groups + LANES]
    v_ref[:, groups + LANES :] = v_ref[:, LANES : 2 * LANES]
    per_row = narrow * slots
    window = per_row + 10 * slots
    here = LANES - used
    for w in range(wide):
        start = LANES + w * per_row - 5 * slots
        zero = v_ref[0:8, start : start + window]
        one = v_ref[8:16, start : start + window]
        own = o_ref[8 * w : 8 * w + 8, :used]
        out_ref[16 * w : 16 * w + 8, :] = jnp.concatenate([own, one[:, :here]], 1)
        rest = jnp.zeros((8, LANES - window - (window - here)), F32)
        out_ref[16 * w + 8 : 16 * w + 16, :] = jnp.concatenate([zero, one[:, here:], rest], 1)


def forward_rows(wide, narrow, x_ref, out_ref):
    per = wide // narrow
    low = jnp.zeros((8, LANES), F32)
    top = jnp.zeros((8, LANES), F32)
    for w in range(wide):
        tile = x_ref[16 * w : 16 * w + 8, :]
        low += tile
        top += x_ref[16 * w + 8 : 16 * w + 16, :]
        row = (w // per) * (8 * per + 16) + 8 * (w % per)
        out_ref[row : row + 8, :] = tile
    for n in range(narrow):
        row = n * (8 * per + 16) + 8 * per
        out_ref[row : row + 8, :] = low
        out_ref[row + 8 : row + 16, :] = top


def unpack(rows_here, chunk, per, narrow, x_ref, out_ref, lo_ref, hi_ref):
    block = 8 * per + 16
    cols = per * rows_here
    length = out_ref.shape[1]
    for r in range(2 * rows_here):
        tiles = [x_ref[pl.ds(n * block + r, per, stride=8), :] for n in range(narrow)]
        for y in range(rows_here):
            pieces = [t[:, chunk * y : chunk * (y + 1)] for t in tiles]
            line = jnp.concatenate(pieces + [jnp.zeros((per, 2 * LANES - length), F32)], 1)
            lo_ref[pl.ds(r * cols + y, per, stride=rows_here), :] = line[:, :LANES]
            hi_ref[pl.ds(r * cols + y, per, stride=rows_here), :] = line[:, LANES:]
    out_ref[:, :LANES] = lo_ref[...]
    out_ref[:, LANES:] = hi_ref[:, : length - LANES]


def sweeps(
    slots, narrow, per, used, place_ref, count_ref, near_ref, recv_ref, before_ref, row_ref, after_ref,
    left_ref, mid_h, mid_l, last_h, last_l, out_ref, one_ref, two_ref, high_ref, low_ref, edge_ref, edge_smem, sem,
):
    block = 8 * per + 16
    window = narrow * slots + 10 * slots
    here = LANES - used
    low = jnp.zeros((8, LANES), F32)
    top = jnp.zeros((8, LANES), F32)
    for n in range(narrow):
        row = n * block + 8 * per
        low += recv_ref[row : row + 8, :]
        top += recv_ref[row + 8 : row + 16, :]
    edge_ref[0:8, :] = top
    edge_ref[8:16, :] = jnp.concatenate(
        [low[:, used:], top[:, window : 2 * window - here], jnp.zeros((8, LANES - window), F32)], 1
    )
    copy = pltpu.make_async_copy(edge_ref, edge_smem, sem)
    copy.start()
    mine = place_ref[1]
    total = 2 * REACH + 1
    for r in range(total):
        at = mine + r + narrow - REACH

        @pl.when(at < narrow)
        def _(r=r, at=at):
            one_ref[slots * r : slots * (r + 1)] = before_ref[at - (narrow - REACH), :, 0 : 2 * EDGE, :]

        @pl.when((at >= narrow) & (at < 2 * narrow))
        def _(r=r, at=at):
            one_ref[slots * r : slots * (r + 1)] = row_ref[at - narrow, :, 0 : 2 * EDGE, :]

        @pl.when(at >= 2 * narrow)
        def _(r=r, at=at):
            one_ref[slots * r : slots * (r + 1)] = after_ref[at - 2 * narrow, :, 0 : 2 * EDGE, :]

    copy.wait()
    rows = lax.broadcasted_iota(jnp.int32, (2 * EDGE, CELLS), 0)
    lanes = lax.broadcasted_iota(jnp.int32, (2 * EDGE, CELLS), 1)
    real = rows < EDGE
    upper_half = (rows % EDGE >= 8, lanes >= CELLS // 2, lanes % EDGE >= 8)
    tables = (None, (mid_h, mid_l), (last_h, last_l))
    held = [one_ref, two_ref]
    for s in range(3 * SUBCYCLES):
        k = s % 3
        source, target = held[s % 2], held[1 - s % 2]
        first, end = slots * (s + 1), slots * (total - s - 1)

        def ghost(q, face, source=source):
            near = near_ref[q * 6 + face]
            lane = q + slots * (mine - 1)
            flat = jnp.where(real, edge_smem[face, lane], edge_smem[8 + face, lane])
            return jnp.where(near >= 0, source[jnp.maximum(near, 0)], flat)

        def gather(q, k=k, source=source, ghost=ghost):
            return source[q], jnp.where(upper_half[k], ghost(q, 2 * k), ghost(q, 2 * k + 1))

        if k == 0:

            def step(q, carry, gather=gather, target=target):
                high, low_ = split(jnp.concatenate(gather(q), 0))
                target[q] = mm(left_ref[...], jnp.concatenate([high, low_, high], 0))
                return carry

            lax.fori_loop(first, end, step, 0, unroll=4)
        else:
            wh, wl = tables[k]

            def step(d, carry, gather=gather, target=target, wh=wh, wl=wl):
                for i in range(slots):
                    high, low_ = split(jnp.concatenate(gather(slots * d + i), 1))
                    high_ref[2 * EDGE * i : 2 * EDGE * (i + 1), :] = high
                    low_ref[2 * EDGE * i : 2 * EDGE * (i + 1), :] = low_
                done = mm3((high_ref[...], low_ref[...]), (wh[...], wl[...]))
                for i in range(slots):
                    a, b = 2 * EDGE * i, 2 * EDGE * i + EDGE
                    re, im = done[a:b], done[b : b + EDGE]
                    target[slots * d + i, 0:EDGE, :] = re[:, :CELLS] - im[:, CELLS:]
                    target[slots * d + i, EDGE:, :] = im[:, :CELLS] + re[:, CELLS:]
                return carry

            lax.fori_loop(first // slots, end // slots, step, 0)
    final = held[0]
    for i in range(slots):
        value = final[slots * REACH + i]
        out_ref[i] = jnp.where(i < count_ref[0], value, jnp.zeros_like(value))


def shifted(block, axis, distance):
    devices = range(lax.axis_size(axis))
    route = [((i - distance) % len(devices), i) for i in devices]
    return lax.ppermute(block, axis, route)


def call(kernel, out_rows, out_cols, specs, scratch=()):
    return pl.pallas_call(
        kernel,
        out_shape=jax.ShapeDtypeStruct((out_rows, out_cols), F32),
        in_specs=specs,
        out_specs=VMEM,
        scratch_shapes=list(scratch),
        compiler_params=PARAMS,
    )


def exchange(block, axis):
    parts = lax.axis_size(axis)
    shape = (parts, block.shape[0] // parts, block.shape[1])
    return lax.all_to_all(block.reshape(shape), axis, split_axis=0, concat_axis=0, tiled=True).reshape(block.shape)


def shards(base, fine_psi, counts, neighbors, base_cell):
    wide = lax.axis_size("wide")
    narrow = lax.axis_size("narrow")
    w_at = lax.axis_index("wide")
    n_at = lax.axis_index("narrow")
    _, rows_here, cols_here, length = base.shape
    slots = fine_psi.shape[0]
    chunk = length // narrow
    per = wide // narrow
    used = rows_here * chunk
    place = jnp.stack([w_at, n_at]).astype(jnp.int32)

    numbers = jnp.pad(neighbors.astype(F32)[:, None, :], ((0, 0), (0, 7), (0, CELLS - 6)))
    packet = jnp.concatenate([fine_psi.reshape(slots, 2 * EDGE, CELLS), numbers], 1)
    row = lax.all_gather(packet, "narrow", axis=0, tiled=False)
    before = shifted(row[narrow - REACH :], "wide", 1)
    after = shifted(row[:REACH], "wide", -1)

    kr, ki = circulant(length)
    first_axis = [jnp.asarray(t) for m in (kr, ki) for t in two_parts(m)]
    sent = call(
        lambda *refs: along_last(rows_here, cols_here, narrow, *refs), narrow * 2 * cols_here, LANES, [VMEM] * 5
    )(base.reshape(2 * rows_here * cols_here, length), *first_axis)
    got = exchange(sent, "narrow")

    full = np.stack([np.stack([kr, -ki]), np.stack([ki, kr])])
    second = full.reshape(2, 2, wide, rows_here, narrow, cols_here).transpose(0, 3, 2, 4, 1, 5)
    second = second.reshape(2 * length, 2 * length)
    sent = call(lambda *refs: along_second(rows_here, chunk, wide, *refs), wide * 8, LANES, [VMEM] * 3)(
        got, *[jnp.asarray(t) for t in two_parts(second)]
    )
    got = exchange(sent, "wide")

    third = np.zeros((wide, 8, wide, 8))
    blocks = full.reshape(2, 2, wide, rows_here, wide, rows_here).transpose(2, 0, 3, 4, 1, 5)
    third[:, : 2 * rows_here, :, : 2 * rows_here] = blocks.reshape(wide, 2 * rows_here, wide, 2 * rows_here)
    third = third.reshape(wide * 8, wide * 8)
    cells = jnp.transpose(base_cell, (2, 1, 0)).reshape(18, base_cell.shape[0])
    sent = call(
        lambda *refs: along_first(rows_here, chunk, wide, narrow, slots, *refs),
        wide * 16,
        LANES,
        [SMEM] + [VMEM] * 4,
        [pltpu.VMEM((wide * 8, LANES), F32), pltpu.VMEM((16, base_cell.shape[0] + 2 * LANES), F32)],
    )(place, cells, got, *[jnp.asarray(t) for t in two_parts(third)])
    got = exchange(sent, "wide")
    sent = call(lambda *refs: forward_rows(wide, narrow, *refs), narrow * (8 * per + 16), LANES, [VMEM])(got)
    got = exchange(sent, "narrow")
    drifted = call(
        lambda *refs: unpack(rows_here, chunk, per, narrow, *refs), 2 * rows_here * cols_here, length, [VMEM],
        [pltpu.VMEM((2 * rows_here * cols_here, LANES), F32)] * 2,
    )(got)

    devices = wide * narrow
    mine = w_at * narrow + n_at
    numbers = jnp.concatenate([before[:, :, 2 * EDGE, :6], row[:, :, 2 * EDGE, :6], after[:, :, 2 * EDGE, :6]], 0)
    total = 2 * REACH + 1
    numbers = lax.dynamic_slice_in_dim(numbers, n_at, total, 0).astype(jnp.int32)
    owner = numbers // slots
    relative = (owner - mine + REACH + devices) % devices
    near = jnp.where(numbers >= 0, relative * slots + numbers - owner * slots, -1)
    near = jnp.where(near < total * slots, near, -1).reshape(-1)
    tables = [jnp.asarray(t) for t in sweep_tables()]
    fine = pl.pallas_call(
        lambda *refs: sweeps(slots, narrow, per, used, *refs),
        out_shape=jax.ShapeDtypeStruct((slots, 2 * EDGE, CELLS), F32),
        in_specs=[SMEM] * 3 + [VMEM] * 9,
        out_specs=VMEM,
        scratch_shapes=[
            pltpu.VMEM((total * slots, 2 * EDGE, CELLS), F32),
            pltpu.VMEM((total * slots, 2 * EDGE, CELLS), F32),
            pltpu.VMEM((slots * 2 * EDGE, 2 * CELLS), BF16),
            pltpu.VMEM((slots * 2 * EDGE, 2 * CELLS), BF16),
            pltpu.VMEM((16, LANES), F32),
            pltpu.SMEM((16, LANES), F32),
            pltpu.SemaphoreType.DMA,
        ],
        compiler_params=PARAMS,
    )(place, counts, near, got, before, row, after, *tables)
    return (drifted.reshape(base.shape), fine.reshape(fine_psi.shape))


def solution(mesh):
    in_specs = (
        P(None, "wide", "narrow", None),
        P(("wide", "narrow"), None, None, None),
        P(("wide", "narrow")),
        P(("wide", "narrow"), None),
        P(),
    )
    out_specs = (P(None, "wide", "narrow", None), P(("wide", "narrow"), None, None, None))
    return jax.shard_map(shards, mesh=mesh, in_specs=in_specs, out_specs=out_specs, check_vma=False)
```

```python
import jax
import jax.numpy as jnp
import ml_dtypes
import numpy as np
from jax import lax
from jax.experimental import pallas as pl
from jax.experimental.pallas import tpu as pltpu
from jax.sharding import PartitionSpec as P

SUBCYCLES = 2
PHASE_RATE = 8.0
TAYLOR_STEP = 0.6
EDGE = 16
CELLS = EDGE * EDGE
LANES = 128
REACH = 6
VMEM = pl.BlockSpec(memory_space=pltpu.VMEM)
SMEM = pl.BlockSpec(memory_space=pltpu.SMEM)
PARAMS = pltpu.CompilerParams(vmem_limit_bytes=48 * 2**20)
F32 = jnp.float32
BF16 = jnp.bfloat16


def two_parts(matrix):
    high = matrix.astype(ml_dtypes.bfloat16)
    low = (matrix - high.astype(np.float64)).astype(ml_dtypes.bfloat16)
    return high, low


def circulant(length):
    signed = np.fft.fftfreq(length, 1.0 / length)
    phase = np.exp(-1j * PHASE_RATE * (2.0 * np.pi * signed / length) ** 2)
    kernel = np.fft.ifft(phase)
    index = np.arange(length)
    matrix = kernel[(index[:, None] - index[None, :]) % length]
    return matrix.real, matrix.imag


def stacked(*matrices):
    return np.concatenate([part for m in matrices for part in two_parts(m)], 0)


def sweep_tables():
    laplace = -2.0 * np.eye(24) + np.eye(24, k=1) + np.eye(24, k=-1)
    squared = laplace @ laplace
    c = TAYLOR_STEP
    real = np.eye(24) - c**2 / 2.0 * squared + c**4 / 24.0 * squared @ squared
    imag = c * laplace - c**3 / 6.0 * squared @ laplace
    own, ghost, half = [], [], []
    for rows in (real[4:20], imag[4:20]):
        assert np.allclose(rows[:8, :16], rows[8:, 8:])
        edge = np.zeros((EDGE, EDGE))
        edge[:, 12:] = rows[:, :4]
        edge[:, :4] = rows[:, 20:]
        own.append(rows[:, 4:20])
        ghost.append(edge)
        half.append(np.concatenate([rows[:8, 4:16], rows[:8, :4]], 1))
    left = [np.block([[t[0], -t[1]], [t[1], t[0]]]) for t in (own, ghost)]
    high, low = two_parts(np.concatenate(left, 1))
    pad = np.zeros((2 * EDGE, CELLS - 12 * EDGE), high.dtype)
    left = np.concatenate([high, high, low, pad], 1)
    middle = np.concatenate([np.kron(t.T, np.eye(EDGE)) for t in half], 1)
    last = np.block([[np.kron(np.eye(8), t[i].T) for i in range(2)] for t in (own, ghost)])
    return np.concatenate([stacked(middle, last), left], 0)


def split(values):
    high = values.astype(BF16)
    return high, (values - high.astype(F32)).astype(BF16)


def halves(table_ref, index):
    size = table_ref.shape[1]
    start = 2 * size * index
    return table_ref[start : start + size, :], table_ref[start + size : start + 2 * size, :]


def mm(a, b):
    return jnp.dot(a, b, preferred_element_type=F32)


def mm3(a, b):
    return mm(a[0], b[0]) + (mm(a[1], b[0]) + mm(a[0], b[1]))


def packed(tiles):
    used = tiles[0].shape[1]
    room = LANES - used
    pad = jnp.zeros((tiles[0].shape[0], 2 * room - used), tiles[0].dtype)
    extra = [t[:, :room] for t in tiles[4:]] + [jnp.concatenate([t[:, room:], pad], 1) for t in tiles[4:]]
    return [jnp.concatenate([t, e], 1) for t, e in zip(tiles[:4], extra, strict=True)]


def unpacked(rows, used):
    room = LANES - used
    extra = [jnp.concatenate([rows[i][:, used:], rows[2 + i][:, used : 2 * used - room]], 1) for i in range(2)]
    return [t[:, :used] for t in rows] + extra


def along_last(rows_here, cols_here, parts, base_ref, near_ref, table_ref, out_ref):
    plane = rows_here * cols_here
    x = split(base_ref[...])
    pr = mm3(x, halves(table_ref, 0))
    pi = mm3(x, halves(table_ref, 1))
    done = (pr[:plane] - pi[plane:], pi[:plane] + pr[plane:])
    chunk = done[0].shape[1] // parts
    near = near_ref[...].astype(F32)
    near = jnp.concatenate([near, jnp.zeros((8 - near.shape[0], near.shape[1]), F32)], 0)
    free = LANES - cols_here // 8 * chunk
    near = jnp.concatenate([near, jnp.zeros((8, free - near.shape[1]), F32)], 1)
    pad = jnp.zeros((cols_here, LANES - (2 * rows_here - 1) * chunk), F32)
    for n in range(parts):
        pieces = [
            done[p][cols_here * x : cols_here * (x + 1), chunk * n : chunk * (n + 1)]
            for p in range(2)
            for x in range(rows_here)
        ]
        at = (cols_here + 8) * n
        out_ref[at : at + cols_here, :] = jnp.concatenate(pieces[:-1] + [pad], 1)
        last = [pieces[-1][8 * i : 8 * i + 8] for i in range(cols_here // 8)]
        out_ref[at + cols_here : at + cols_here + 8, :] = jnp.concatenate(last + [near], 1)


def along_second(rows_here, chunk, wide, narrow, x_ref, table_ref, out_ref):
    cols_here = x_ref.shape[0] // narrow - 8
    used = rows_here * chunk
    real = [x_ref[(cols_here + 8) * n : (cols_here + 8) * n + cols_here, :] for n in range(narrow)]
    real = jnp.concatenate(real, 0)
    last = []
    for n in range(narrow):
        tile = x_ref[(cols_here + 8) * n + cols_here : (cols_here + 8) * (n + 1), :]
        last += [tile[:, chunk * i : chunk * (i + 1)] for i in range(cols_here // 8)]
    last = jnp.concatenate(last, 0)
    pad = jnp.zeros((last.shape[0], LANES - used), F32)
    imag = jnp.concatenate([real[:, used : 2 * used - chunk], last, pad], 1)
    done = mm3(halves(table_ref, 0), split(jnp.concatenate([real, imag], 0)))
    tiles = []
    for p in range(2):
        for x in range(rows_here):
            pieces = [
                done[(p * rows_here + j) * wide : (p * rows_here + j + 1) * wide, chunk * x : chunk * (x + 1)]
                for j in range(rows_here)
            ]
            tiles.append(jnp.concatenate(pieces, 1))
    for q, row in enumerate(packed(tiles)):
        out_ref[pl.ds(q, wide, stride=4), :] = row


def plan(rows_here, chunk, wide, place_ref, cell_ref, line_ref, lane_ref, flag_ref):
    groups = cell_ref.shape[1]
    first = cell_ref[0:6, :]
    second = cell_ref[6:12, :] - place_ref[0] * rows_here
    last = cell_ref[12:18, :] - place_ref[1] * chunk
    mine = (second >= 0) & (second < rows_here) & (last >= 0) & (last < chunk)
    owner = first // rows_here
    lane = jnp.where(mine, second * chunk + last, -1)
    line_ref[0:6, :] = (first - owner * rows_here) * wide + owner
    lane_ref[0:6, :] = lane
    flag_ref[...] = jnp.full_like(flag_ref[...], -1)
    for c in range(groups // LANES):
        flag_ref[0:6, c : c + 1] = jnp.max(lane[:, LANES * c : LANES * (c + 1)], axis=1, keepdims=True)


def along_first(
    rows_here, chunk, wide, narrow, slots, flag_ref, line_ref, lane_ref, first_ref, x_ref, table_ref, out_ref, v_ref, left_ref
):
    used = rows_here * chunk
    lines = rows_here * wide
    groups = line_ref.shape[1]
    rows = [x_ref[pl.ds(q, wide, stride=4), :] for q in range(4)]
    blank = jnp.zeros((wide, LANES - used), F32)
    extra = [jnp.concatenate([t, blank], 1) for t in unpacked(rows, used)[4:]]
    done = mm3(halves(table_ref, 0), split(jnp.concatenate([x_ref[...]] + extra, 0)))
    turned = []
    for p in range(2):
        natural = [done[p * lines : (p + 1) * lines], jnp.zeros((256 - lines, LANES), F32)]
        turned.append(jnp.concatenate(natural, 0).T[:used])
    high, low = split(jnp.concatenate(turned, 0))
    left_ref[...] = jnp.concatenate([high, low], 0)
    v_ref[...] = jnp.zeros_like(v_ref[...])
    step = LANES

    def body(c, carry):
        at = pl.multiple_of(c * step, step)
        for f in range(6):

            @pl.when(flag_ref[f, c] >= 0)
            def _(f=f):
                line_of = lax.broadcasted_iota(jnp.int32, (256, step), 0)
                lane_of = lax.broadcasted_iota(jnp.int32, (used, step), 0)
                hot = jnp.where(line_of == line_ref[f : f + 1, pl.ds(at, step)], 1.0, 0.0).astype(BF16)
                taken = mm(left_ref[...], hot)
                keep = lane_of == lane_ref[f : f + 1, pl.ds(at, step)]
                for p in range(2):
                    both = taken[p * used : (p + 1) * used] + taken[(2 + p) * used : (3 + p) * used]
                    v_ref[4 + 6 * p + f : 5 + 6 * p + f, pl.ds(at + LANES, step)] = jnp.sum(
                        jnp.where(keep, both, 0.0), axis=0, keepdims=True
                    )

        return carry

    lax.fori_loop(0, groups // step, body, 0)
    v_ref[:, :LANES] = v_ref[:, groups : groups + LANES]
    v_ref[:, groups + LANES :] = v_ref[:, LANES : 2 * LANES]
    per_row = narrow * slots
    window = per_row + 10 * slots
    block = first_ref.shape[0] // narrow
    near = [
        first_ref[block * n + block - 8 : block * (n + 1), (block - 8) // 8 * chunk : (block - 8) // 8 * chunk + 6]
        for n in range(narrow)
    ]
    near = jnp.concatenate([t[:slots] for t in near], 1)
    near = jnp.concatenate([near, jnp.zeros((slots, LANES - window - near.shape[1]), F32)], 1)
    near = jnp.concatenate([jnp.zeros((4, LANES - window), F32), near, jnp.zeros((8, LANES - window), F32)], 0)
    for w in range(wide):
        start = LANES + w * per_row - 5 * slots
        out_ref[16 * w : 16 * w + 16, :] = jnp.concatenate([v_ref[:, start : start + window], near], 1)
    tiles = [done[wide * r : wide * (r + 1), :used] for r in range(2 * rows_here)]
    for q, row in enumerate(packed(tiles)):
        out_ref[pl.ds(q, wide, stride=16), :] = row


def forward_rows(slots, wide, narrow, place_ref, x_ref, out_ref, near_ref):
    per = wide // narrow
    block = 4 * per + 16
    low = jnp.zeros((8, LANES), F32)
    top = jnp.zeros((8, LANES), F32)
    for w in range(0, wide, 2):
        one = x_ref[16 * w : 16 * w + 8, :]
        two = x_ref[16 * w + 16 : 16 * w + 24, :]
        low += one + two
        top += x_ref[16 * w + 8 : 16 * w + 16, :] + x_ref[16 * w + 24 : 16 * w + 32, :]
        row = w // per * block + 4 * (w % per)
        out_ref[row : row + 8, :] = jnp.concatenate([one[:4], two[:4]], 0)
    for n in range(narrow):
        row = n * block + 4 * per
        out_ref[row : row + 8, :] = low
        out_ref[row + 8 : row + 16, :] = top
    devices = wide * narrow
    mine = place_ref[0] * narrow + place_ref[1]
    for o in range(3):
        at = lax.rem(place_ref[0] + (o - 1 + wide), wide) * 16
        numbers = x_ref[pl.ds(pl.multiple_of(at, 16), 8), :].astype(jnp.int32)
        owner = jnp.maximum(numbers, 0) // slots
        away = owner - mine + REACH
        away = jnp.where(away < 0, away + devices, away)
        away = jnp.where(away >= devices, away - devices, away)
        known = (numbers >= 0) & (away <= 2 * REACH)
        near_ref[8 * o : 8 * o + 8, :] = jnp.where(known, (away - owner) * slots + numbers, -1)


def unpack(rows_here, chunk, per, narrow, x_ref, out_ref, lo_ref, hi_ref):
    block = 4 * per + 16
    cols = per * rows_here
    length = out_ref.shape[1]
    tiles = [
        unpacked([x_ref[pl.ds(n * block + q, per, stride=4), :] for q in range(4)], rows_here * chunk)
        for n in range(narrow)
    ]
    for r in range(2 * rows_here):
        for y in range(rows_here):
            pieces = [t[r][:, chunk * y : chunk * (y + 1)] for t in tiles]
            line = jnp.concatenate(pieces + [jnp.zeros((per, 2 * LANES - length), F32)], 1)
            lo_ref[pl.ds(r * cols + y, per, stride=rows_here), :] = line[:, :LANES]
            hi_ref[pl.ds(r * cols + y, per, stride=rows_here), :] = line[:, LANES:]
    out_ref[:, :LANES] = lo_ref[...]
    out_ref[:, LANES:] = hi_ref[:, : length - LANES]


def sweeps(
    slots, narrow, per, used, place_ref, count_ref, near_ref, recv_ref, before_ref, row_ref, after_ref,
    table_ref, out_ref, one_ref, two_ref, edge_ref, edge_smem, sem,
):
    block = 4 * per + 16
    low = jnp.zeros((8, LANES), F32)
    top = jnp.zeros((8, LANES), F32)
    for n in range(narrow):
        row = n * block + 4 * per
        low += recv_ref[row : row + 8, :]
        top += recv_ref[row + 8 : row + 16, :]
    edge_ref[0:8, :] = low
    edge_ref[8:16, :] = top
    copy = pltpu.make_async_copy(edge_ref, edge_smem, sem)
    copy.start()
    mine = place_ref[1]
    total = 2 * REACH + 1
    for r in range(total):
        at = mine + r + narrow - REACH

        @pl.when(at < narrow)
        def _(r=r, at=at):
            one_ref[slots * r : slots * (r + 1)] = before_ref[at - (narrow - REACH)]

        @pl.when((at >= narrow) & (at < 2 * narrow))
        def _(r=r, at=at):
            one_ref[slots * r : slots * (r + 1)] = row_ref[at - narrow]

        @pl.when(at >= 2 * narrow)
        def _(r=r, at=at):
            one_ref[slots * r : slots * (r + 1)] = after_ref[at - 2 * narrow]

    copy.wait()
    row = lax.broadcasted_iota(jnp.int32, (2 * EDGE, CELLS), 0)
    real = row < EDGE
    late_row = row % EDGE >= 8
    column = lax.broadcasted_iota(jnp.int32, (2 * EDGE, LANES), 1)
    real_half = real[:, :LANES]
    early_half = column < LANES // 2
    late_last = column % EDGE >= 8
    left = table_ref[4 * CELLS :, : 12 * EDGE]
    held = [one_ref, two_ref]
    for s in range(3 * SUBCYCLES):
        k = s % 3
        source, target = held[s % 2], held[1 - s % 2]
        first, end = slots * (s + 1), slots * (total - s - 1)

        def ghost(q, face, part, is_real, source=source):
            at = q // slots + mine + narrow - REACH
            near = near_ref[at // narrow * 8 + 4 + q % slots, used + 6 * (at % narrow) + face]
            lane = q + slots * (mine - 1)
            flat = jnp.where(is_real, edge_smem[4 + face, lane], edge_smem[10 + face, lane])
            return jnp.where(near >= 0, source[jnp.maximum(near, 0), :, part], flat)

        if k == 0:

            def step(q, carry, source=source, target=target, ghost=ghost):
                every = slice(0, CELLS)
                around = jnp.where(late_row, ghost(q, 0, every, real), ghost(q, 1, every, real))
                high, rest = split(jnp.concatenate([source[q], around], 0))
                target[q] = mm(left, jnp.concatenate([high, rest, high], 0))
                return carry

            lax.fori_loop(first, end, step, 0, unroll=4)
        else:
            table = halves(table_ref, k - 1)

            def step(d, carry, k=k, source=source, target=target, ghost=ghost, table=table):
                lower, upper = slice(0, LANES), slice(LANES, CELLS)
                lines = []
                for i in range(slots):
                    q = slots * d + i
                    near, far = source[q, :, lower], source[q, :, upper]
                    if k == 1:
                        before = ghost(q, 2, upper, real_half)
                        after = ghost(q, 3, lower, real_half)
                        sides = jnp.where(early_half, far, before), jnp.where(early_half, after, near)
                    else:
                        sides = [
                            jnp.where(late_last, ghost(q, 4, part, real_half), ghost(q, 5, part, real_half))
                            for part in (lower, upper)
                        ]
                    lines += [jnp.concatenate([near, sides[0]], 1), jnp.concatenate([far, sides[1]], 1)]
                done = mm3(split(jnp.concatenate(lines, 0)), table)
                for i in range(slots):
                    for part, at in ((lower, 4 * EDGE * i), (upper, 4 * EDGE * i + 2 * EDGE)):
                        re, im = done[at : at + EDGE], done[at + EDGE : at + 2 * EDGE]
                        target[slots * d + i, 0:EDGE, part] = re[:, :LANES] - im[:, LANES:]
                        target[slots * d + i, EDGE:, part] = im[:, :LANES] + re[:, LANES:]
                return carry

            lax.fori_loop(first // slots, end // slots, step, 0)
    final = held[0]
    for i in range(slots):
        value = final[slots * REACH + i]
        out_ref[i] = jnp.where(i < count_ref[0], value, jnp.zeros_like(value))


def shifted(block, axis, distance):
    devices = range(lax.axis_size(axis))
    route = [((i - distance) % len(devices), i) for i in devices]
    return lax.ppermute(block, axis, route)


def call(kernel, outs, specs, scratch=()):
    return pl.pallas_call(
        kernel,
        out_shape=[jax.ShapeDtypeStruct(shape, dtype) for shape, dtype in outs],
        in_specs=specs,
        out_specs=[VMEM] * len(outs),
        scratch_shapes=list(scratch),
        compiler_params=PARAMS,
    )


def exchange(block, axis):
    parts = lax.axis_size(axis)
    shape = (parts, block.shape[0] // parts, block.shape[1])
    return lax.all_to_all(block.reshape(shape), axis, split_axis=0, concat_axis=0, tiled=True).reshape(block.shape)


def shards(base, fine_psi, counts, neighbors, base_cell):
    wide = lax.axis_size("wide")
    narrow = lax.axis_size("narrow")
    w_at = lax.axis_index("wide")
    n_at = lax.axis_index("narrow")
    _, rows_here, cols_here, length = base.shape
    slots = fine_psi.shape[0]
    chunk = length // narrow
    per = wide // narrow
    used = rows_here * chunk
    place = jnp.stack([w_at, n_at]).astype(jnp.int32)

    row = lax.all_gather(fine_psi.reshape(slots, 2 * EDGE, CELLS), "narrow", axis=0, tiled=False)
    before = shifted(row[narrow - REACH :], "wide", 1)
    after = shifted(row[:REACH], "wide", -1)

    kr, ki = circulant(length)
    (sent,) = call(
        lambda *refs: along_last(rows_here, cols_here, narrow, *refs),
        [((narrow * (cols_here + 8), LANES), F32)],
        [VMEM] * 3,
    )(base.reshape(2 * rows_here * cols_here, length), neighbors, jnp.asarray(stacked(kr, ki)))
    first = exchange(sent, "narrow")

    full = np.stack([np.stack([kr, -ki]), np.stack([ki, kr])])
    second = full.transpose(0, 2, 1, 3).reshape(2, wide, rows_here, 2 * length).transpose(0, 2, 1, 3)
    second = stacked(second.reshape(2 * length, 2 * length))
    (sent,) = call(
        lambda *refs: along_second(rows_here, chunk, wide, narrow, *refs), [((wide * 4, LANES), F32)], [VMEM] * 2
    )(first, jnp.asarray(second))
    groups = base_cell.shape[0]
    cells = jnp.transpose(base_cell, (2, 1, 0)).reshape(18, groups)
    line, lane, flags = call(
        lambda *refs: plan(rows_here, chunk, wide, *refs),
        [((8, groups), jnp.int32), ((8, groups), jnp.int32), ((8, LANES), jnp.int32)],
        [SMEM, VMEM],
    )(place, cells)

    got = exchange(sent, "wide")
    third = full.reshape(2, 2, wide, rows_here, wide, rows_here).transpose(0, 3, 2, 1, 5, 4)
    third = third.reshape(2 * length, 2 * rows_here, wide)
    main = third[:, :4].transpose(0, 2, 1).reshape(2 * length, 4 * wide)
    third = stacked(np.concatenate([main, third[:, 4:].reshape(2 * length, 2 * wide)], 1))
    (sent,) = call(
        lambda *refs: along_first(rows_here, chunk, wide, narrow, slots, *refs),
        [((wide * 16, LANES), F32)],
        [SMEM] + [VMEM] * 5,
        [pltpu.VMEM((16, groups + 2 * LANES), F32), pltpu.VMEM((4 * used, 256), BF16)],
    )(flags, line, lane, first, got, jnp.asarray(third))
    got = exchange(sent, "wide")
    sent, near = call(
        lambda *refs: forward_rows(slots, wide, narrow, *refs),
        [((narrow * (4 * per + 16), LANES), F32), ((24, LANES), jnp.int32)],
        [SMEM, VMEM],
    )(place, got)
    got = exchange(sent, "narrow")
    (drifted,) = call(
        lambda *refs: unpack(rows_here, chunk, per, narrow, *refs),
        [((2 * rows_here * cols_here, length), F32)],
        [VMEM],
        [pltpu.VMEM((2 * rows_here * cols_here, LANES), F32)] * 2,
    )(got)

    total = 2 * REACH + 1
    (fine,) = call(
        lambda *refs: sweeps(slots, narrow, per, used, *refs),
        [((slots, 2 * EDGE, CELLS), F32)],
        [SMEM] * 3 + [VMEM] * 5,
        [
            pltpu.VMEM((total * slots, 2 * EDGE, CELLS), F32),
            pltpu.VMEM((total * slots, 2 * EDGE, CELLS), F32),
            pltpu.VMEM((16, LANES), F32),
            pltpu.SMEM((16, LANES), F32),
            pltpu.SemaphoreType.DMA,
        ],
    )(place, counts, near, got, before, row, after, jnp.asarray(sweep_tables()))
    return (drifted.reshape(base.shape), fine.reshape(fine_psi.shape))


def solution(mesh):
    in_specs = (
        P(None, "wide", "narrow", None),
        P(("wide", "narrow"), None, None, None),
        P(("wide", "narrow")),
        P(("wide", "narrow"), None),
        P(),
    )
    out_specs = (P(None, "wide", "narrow", None), P(("wide", "narrow"), None, None, None))
    return jax.shard_map(shards, mesh=mesh, in_specs=in_specs, out_specs=out_specs, check_vma=False)
```

```python
import jax
import jax.numpy as jnp
import ml_dtypes
import numpy as np
from jax import lax
from jax.experimental import pallas as pl
from jax.experimental.pallas import tpu as pltpu
from jax.sharding import PartitionSpec as P

SUBCYCLES = 2
PHASE_RATE = 8.0
TAYLOR_STEP = 0.6
EDGE = 16
CELLS = EDGE * EDGE
LANES = 128
REACH = 6
VMEM = pl.BlockSpec(memory_space=pltpu.VMEM)
SMEM = pl.BlockSpec(memory_space=pltpu.SMEM)
PARAMS = pltpu.CompilerParams(vmem_limit_bytes=48 * 2**20)
F32 = jnp.float32
BF16 = jnp.bfloat16


def two_parts(matrix):
    high = matrix.astype(ml_dtypes.bfloat16)
    low = (matrix - high.astype(np.float64)).astype(ml_dtypes.bfloat16)
    return high, low


def circulant(length):
    signed = np.fft.fftfreq(length, 1.0 / length)
    phase = np.exp(-1j * PHASE_RATE * (2.0 * np.pi * signed / length) ** 2)
    kernel = np.fft.ifft(phase)
    index = np.arange(length)
    matrix = kernel[(index[:, None] - index[None, :]) % length]
    return matrix.real, matrix.imag


def stacked(*matrices):
    return np.concatenate([part for m in matrices for part in two_parts(m)], 0)


def sweep_tables():
    laplace = -2.0 * np.eye(24) + np.eye(24, k=1) + np.eye(24, k=-1)
    squared = laplace @ laplace
    c = TAYLOR_STEP
    real = np.eye(24) - c**2 / 2.0 * squared + c**4 / 24.0 * squared @ squared
    imag = c * laplace - c**3 / 6.0 * squared @ laplace
    own, ghost, half = [], [], []
    for rows in (real[4:20], imag[4:20]):
        assert np.allclose(rows[:8, :16], rows[8:, 8:])
        edge = np.zeros((EDGE, EDGE))
        edge[:, 12:] = rows[:, :4]
        edge[:, :4] = rows[:, 20:]
        own.append(rows[:, 4:20])
        ghost.append(edge)
        half.append(np.concatenate([rows[:8, 4:16], rows[:8, :4]], 1))
    left = [np.block([[t[0], -t[1]], [t[1], t[0]]]) for t in (own, ghost)]
    high, low = two_parts(np.concatenate(left, 1))
    pad = np.zeros((2 * EDGE, CELLS - 12 * EDGE), high.dtype)
    left = np.concatenate([high, high, low, pad], 1)
    middle = np.concatenate([np.kron(t.T, np.eye(EDGE)) for t in half], 1)
    last = np.block([[np.kron(np.eye(8), t[i].T) for i in range(2)] for t in (own, ghost)])
    return np.concatenate([stacked(middle, last), left], 0)


def split(values):
    high = values.astype(BF16)
    return high, (values - high.astype(F32)).astype(BF16)


def halves(table_ref, index):
    size = table_ref.shape[1]
    start = 2 * size * index
    return table_ref[start : start + size, :], table_ref[start + size : start + 2 * size, :]


def mm(a, b):
    return jnp.dot(a, b, preferred_element_type=F32)


def mm3(a, b):
    return mm(a[0], b[0]) + (mm(a[1], b[0]) + mm(a[0], b[1]))


def packed(tiles):
    used = tiles[0].shape[1]
    room = LANES - used
    pad = jnp.zeros((tiles[0].shape[0], 2 * room - used), tiles[0].dtype)
    extra = [t[:, :room] for t in tiles[4:]] + [jnp.concatenate([t[:, room:], pad], 1) for t in tiles[4:]]
    return [jnp.concatenate([t, e], 1) for t, e in zip(tiles[:4], extra, strict=True)]


def unpacked(rows, used):
    room = LANES - used
    extra = [jnp.concatenate([rows[i][:, used:], rows[2 + i][:, used : 2 * used - room]], 1) for i in range(2)]
    return [t[:, :used] for t in rows] + extra


def along_last(rows_here, cols_here, parts, base_ref, near_ref, table_ref, out_ref):
    plane = rows_here * cols_here
    x = split(base_ref[...])
    pr = mm3(x, halves(table_ref, 0))
    pi = mm3(x, halves(table_ref, 1))
    done = (pr[:plane] - pi[plane:], pi[:plane] + pr[plane:])
    chunk = done[0].shape[1] // parts
    near = near_ref[...].astype(F32)
    near = jnp.concatenate([near, jnp.zeros((8 - near.shape[0], near.shape[1]), F32)], 0)
    free = LANES - cols_here // 8 * chunk
    near = jnp.concatenate([near, jnp.zeros((8, free - near.shape[1]), F32)], 1)
    pad = jnp.zeros((cols_here, LANES - (2 * rows_here - 1) * chunk), F32)
    for n in range(parts):
        pieces = [
            done[p][cols_here * x : cols_here * (x + 1), chunk * n : chunk * (n + 1)]
            for p in range(2)
            for x in range(rows_here)
        ]
        at = (cols_here + 8) * n
        out_ref[at : at + cols_here, :] = jnp.concatenate(pieces[:-1] + [pad], 1)
        last = [pieces[-1][8 * i : 8 * i + 8] for i in range(cols_here // 8)]
        out_ref[at + cols_here : at + cols_here + 8, :] = jnp.concatenate(last + [near], 1)


def along_second(rows_here, chunk, wide, narrow, x_ref, table_ref, out_ref):
    cols_here = x_ref.shape[0] // narrow - 8
    used = rows_here * chunk
    real = [x_ref[(cols_here + 8) * n : (cols_here + 8) * n + cols_here, :] for n in range(narrow)]
    real = jnp.concatenate(real, 0)
    last = []
    for n in range(narrow):
        tile = x_ref[(cols_here + 8) * n + cols_here : (cols_here + 8) * (n + 1), :]
        last += [tile[:, chunk * i : chunk * (i + 1)] for i in range(cols_here // 8)]
    last = jnp.concatenate(last, 0)
    pad = jnp.zeros((last.shape[0], LANES - used), F32)
    imag = jnp.concatenate([real[:, used : 2 * used - chunk], last, pad], 1)
    done = mm3(halves(table_ref, 0), split(jnp.concatenate([real, imag], 0)))
    tiles = []
    for p in range(2):
        for x in range(rows_here):
            pieces = [
                done[(p * rows_here + j) * wide : (p * rows_here + j + 1) * wide, chunk * x : chunk * (x + 1)]
                for j in range(rows_here)
            ]
            tiles.append(jnp.concatenate(pieces, 1))
    for q, row in enumerate(packed(tiles)):
        out_ref[pl.ds(q, wide, stride=4), :] = row


def plan(rows_here, chunk, wide, place_ref, cell_ref, data_ref, upto_ref, count_ref):
    groups = cell_ref.shape[1]
    first = cell_ref[0:6, :]
    second = cell_ref[6:12, :] - place_ref[0] * rows_here
    last = cell_ref[12:18, :] - place_ref[1] * chunk
    mine = (second >= 0) & (second < rows_here) & (last >= 0) & (last < chunk)
    owner = first // rows_here
    lane = jnp.where(mine, second * chunk + last, -1).astype(F32)
    line = ((first - owner * rows_here) * wide + owner).astype(F32)
    pad = jnp.full((2, LANES), -1.0, F32)

    def chunks(values):
        parts = [values[:, LANES * c : LANES * (c + 1)] for c in range(groups // LANES)]
        return jnp.concatenate([t for part in parts for t in (part, pad)], 0)

    lane, line = chunks(lane), chunks(line)
    mark = jnp.where(lane >= 0, 1.0, 0.0)
    rows, size = mark.shape
    earlier = lax.broadcasted_iota(jnp.int32, (size, size), 0) <= lax.broadcasted_iota(jnp.int32, (size, size), 1)
    above = lax.broadcasted_iota(jnp.int32, (rows, rows), 1) <= lax.broadcasted_iota(jnp.int32, (rows, rows), 0)
    in_row = mm(mark.astype(BF16), jnp.where(earlier, 1.0, 0.0).astype(BF16))
    in_all = jnp.broadcast_to(jnp.sum(mark, axis=1, keepdims=True), mark.shape)
    upto = mm(jnp.where(above, 1.0, 0.0).astype(BF16), in_all.astype(BF16))
    high, low = split(upto - in_all + in_row)
    upto_ref[...] = upto
    count_ref[...] = upto[rows - 8 :].astype(jnp.int32)
    data_ref[...] = jnp.concatenate([high, low] + [t.astype(BF16) for t in (mark, line, lane)], 1)


def along_first(
    rows_here, chunk, wide, narrow, slots, count_ref, data_ref, upto_ref, first_ref, x_ref, table_ref, out_ref, v_ref
):
    used = rows_here * chunk
    lines = rows_here * wide
    faces = upto_ref.shape[0]
    groups = faces // 8 * LANES
    rows = [x_ref[pl.ds(q, wide, stride=4), :] for q in range(4)]
    blank = jnp.zeros((wide, LANES - used), F32)
    extra = [jnp.concatenate([t, blank], 1) for t in unpacked(rows, used)[4:]]
    done = mm3(halves(table_ref, 0), split(jnp.concatenate([x_ref[...]] + extra, 0)))
    parts = [split(done[p * lines : (p + 1) * lines]) for p in range(2)]
    source = jnp.concatenate([parts[p][i] for i in range(2) for p in range(2)], 1)
    v_ref[...] = jnp.zeros_like(v_ref[...])
    shape = (LANES, LANES)
    row_at = lax.broadcasted_iota(jnp.int32, (faces, LANES), 0)
    deep = lax.broadcasted_iota(jnp.int32, (2 * faces, LANES), 0)
    sub = lax.broadcasted_iota(jnp.int32, shape, 0)
    lane_at = lax.broadcasted_iota(jnp.int32, shape, 1)
    line_at = lax.broadcasted_iota(jnp.int32, (LANES, lines), 1)

    def body(k, carry):
        wanted = (lane_at[:1] + k * LANES).astype(F32)
        row = jnp.sum(jnp.where(upto_ref[...] <= wanted, 1, 0), axis=0, keepdims=True)
        hot = jnp.where(row_at == row, 1.0, 0.0).T.astype(BF16)
        near = mm(hot, data_ref[...])
        rank, mark, line, lane = near[:, :LANES] + near[:, LANES : 2 * LANES], *jnp.split(near[:, 2 * LANES :], 3, 1)
        hit = jnp.where((rank == (sub + k * LANES + 1).astype(F32)) & (mark > 0.5), 1.0, 0.0)
        line = jnp.sum(hit * line, axis=1, keepdims=True).astype(jnp.int32)
        lane = jnp.sum(hit * lane, axis=1, keepdims=True).astype(jnp.int32)
        taken = mm(jnp.where(line_at == line, 1.0, 0.0).astype(BF16), source)
        back = []
        for p in range(2):
            both = taken[:, LANES * p : LANES * (p + 1)] + taken[:, LANES * (p + 2) : LANES * (p + 3)]
            back.append(jnp.sum(jnp.where(lane_at == lane, both, 0.0), axis=1, keepdims=True) * hit)
        high, low = split(jnp.concatenate(back, 0))
        goal = row // 8 * 16 + row % 8 + 4
        spread = jnp.concatenate([jnp.where(deep == goal + 6 * p, 1.0, 0.0).astype(BF16) for p in range(2)], 1)
        values = mm(spread, high) + mm(spread, low)
        for c in range(faces // 8):
            v_ref[:, LANES * (c + 1) : LANES * (c + 2)] += values[16 * c : 16 * (c + 1)]
        return carry

    lax.fori_loop(0, (count_ref[7, 0] + LANES - 1) // LANES, body, 0)
    v_ref[:, :LANES] = v_ref[:, groups : groups + LANES]
    v_ref[:, groups + LANES :] = v_ref[:, LANES : 2 * LANES]
    per_row = narrow * slots
    window = per_row + 10 * slots
    block = first_ref.shape[0] // narrow
    near = [
        first_ref[block * n + block - 8 : block * (n + 1), (block - 8) // 8 * chunk : (block - 8) // 8 * chunk + 6]
        for n in range(narrow)
    ]
    near = jnp.concatenate([t[:slots] for t in near], 1)
    near = jnp.concatenate([near, jnp.zeros((slots, LANES - window - near.shape[1]), F32)], 1)
    near = jnp.concatenate([jnp.zeros((4, LANES - window), F32), near, jnp.zeros((8, LANES - window), F32)], 0)
    for w in range(wide):
        start = LANES + w * per_row - 5 * slots
        out_ref[16 * w : 16 * w + 16, :] = jnp.concatenate([v_ref[:, start : start + window], near], 1)
    tiles = [done[wide * r : wide * (r + 1), :used] for r in range(2 * rows_here)]
    for q, row in enumerate(packed(tiles)):
        out_ref[pl.ds(q, wide, stride=16), :] = row


def forward_rows(slots, wide, narrow, place_ref, x_ref, out_ref, near_ref):
    per = wide // narrow
    block = 4 * per + 16
    low = jnp.zeros((8, LANES), F32)
    top = jnp.zeros((8, LANES), F32)
    for w in range(0, wide, 2):
        one = x_ref[16 * w : 16 * w + 8, :]
        two = x_ref[16 * w + 16 : 16 * w + 24, :]
        low += one + two
        top += x_ref[16 * w + 8 : 16 * w + 16, :] + x_ref[16 * w + 24 : 16 * w + 32, :]
        row = w // per * block + 4 * (w % per)
        out_ref[row : row + 8, :] = jnp.concatenate([one[:4], two[:4]], 0)
    for n in range(narrow):
        row = n * block + 4 * per
        out_ref[row : row + 8, :] = low
        out_ref[row + 8 : row + 16, :] = top
    devices = wide * narrow
    mine = place_ref[0] * narrow + place_ref[1]
    for o in range(3):
        at = lax.rem(place_ref[0] + (o - 1 + wide), wide) * 16
        numbers = x_ref[pl.ds(pl.multiple_of(at, 16), 8), :].astype(jnp.int32)
        owner = jnp.maximum(numbers, 0) // slots
        away = owner - mine + REACH
        away = jnp.where(away < 0, away + devices, away)
        away = jnp.where(away >= devices, away - devices, away)
        known = (numbers >= 0) & (away <= 2 * REACH)
        near_ref[8 * o : 8 * o + 8, :] = jnp.where(known, (away - owner) * slots + numbers, -1)


def unpack(rows_here, chunk, per, narrow, x_ref, out_ref, lo_ref, hi_ref):
    block = 4 * per + 16
    cols = per * rows_here
    length = out_ref.shape[1]
    tiles = [
        unpacked([x_ref[pl.ds(n * block + q, per, stride=4), :] for q in range(4)], rows_here * chunk)
        for n in range(narrow)
    ]
    for r in range(2 * rows_here):
        for y in range(rows_here):
            pieces = [t[r][:, chunk * y : chunk * (y + 1)] for t in tiles]
            line = jnp.concatenate(pieces + [jnp.zeros((per, 2 * LANES - length), F32)], 1)
            lo_ref[pl.ds(r * cols + y, per, stride=rows_here), :] = line[:, :LANES]
            hi_ref[pl.ds(r * cols + y, per, stride=rows_here), :] = line[:, LANES:]
    out_ref[:, :LANES] = lo_ref[...]
    out_ref[:, LANES:] = hi_ref[:, : length - LANES]


def sweeps(
    slots, narrow, per, used, place_ref, count_ref, near_ref, recv_ref, before_ref, row_ref, after_ref,
    table_ref, out_ref, one_ref, two_ref, edge_ref, edge_smem, sem,
):
    block = 4 * per + 16
    low = jnp.zeros((8, LANES), F32)
    top = jnp.zeros((8, LANES), F32)
    for n in range(narrow):
        row = n * block + 4 * per
        low += recv_ref[row : row + 8, :]
        top += recv_ref[row + 8 : row + 16, :]
    edge_ref[0:8, :] = low
    edge_ref[8:16, :] = top
    copy = pltpu.make_async_copy(edge_ref, edge_smem, sem)
    copy.start()
    mine = place_ref[1]
    total = 2 * REACH + 1
    for r in range(total):
        at = mine + r + narrow - REACH

        @pl.when(at < narrow)
        def _(r=r, at=at):
            one_ref[slots * r : slots * (r + 1)] = before_ref[at - (narrow - REACH)]

        @pl.when((at >= narrow) & (at < 2 * narrow))
        def _(r=r, at=at):
            one_ref[slots * r : slots * (r + 1)] = row_ref[at - narrow]

        @pl.when(at >= 2 * narrow)
        def _(r=r, at=at):
            one_ref[slots * r : slots * (r + 1)] = after_ref[at - 2 * narrow]

    copy.wait()
    row = lax.broadcasted_iota(jnp.int32, (2 * EDGE, CELLS), 0)
    real = row < EDGE
    late_row = row % EDGE >= 8
    column = lax.broadcasted_iota(jnp.int32, (2 * EDGE, LANES), 1)
    real_half = real[:, :LANES]
    early_half = column < LANES // 2
    late_last = column % EDGE >= 8
    left = table_ref[4 * CELLS :, : 12 * EDGE]
    held = [one_ref, two_ref]
    for s in range(3 * SUBCYCLES):
        k = s % 3
        source, target = held[s % 2], held[1 - s % 2]
        first, end = slots * (s + 1), slots * (total - s - 1)

        def ghost(q, face, part, is_real, source=source):
            at = q // slots + mine + narrow - REACH
            near = near_ref[at // narrow * 8 + 4 + q % slots, used + 6 * (at % narrow) + face]
            lane = q + slots * (mine - 1)
            flat = jnp.where(is_real, edge_smem[4 + face, lane], edge_smem[10 + face, lane])
            return jnp.where(near >= 0, source[jnp.maximum(near, 0), :, part], flat)

        if k == 0:

            def step(q, carry, source=source, target=target, ghost=ghost):
                every = slice(0, CELLS)
                around = jnp.where(late_row, ghost(q, 0, every, real), ghost(q, 1, every, real))
                high, rest = split(jnp.concatenate([source[q], around], 0))
                target[q] = mm(left, jnp.concatenate([high, rest, high], 0))
                return carry

            lax.fori_loop(first, end, step, 0, unroll=4)
        else:
            table = halves(table_ref, k - 1)

            def step(d, carry, k=k, source=source, target=target, ghost=ghost, table=table):
                lower, upper = slice(0, LANES), slice(LANES, CELLS)
                lines = []
                for i in range(slots):
                    q = slots * d + i
                    near, far = source[q, :, lower], source[q, :, upper]
                    if k == 1:
                        before = ghost(q, 2, upper, real_half)
                        after = ghost(q, 3, lower, real_half)
                        sides = jnp.where(early_half, far, before), jnp.where(early_half, after, near)
                    else:
                        sides = [
                            jnp.where(late_last, ghost(q, 4, part, real_half), ghost(q, 5, part, real_half))
                            for part in (lower, upper)
                        ]
                    lines += [jnp.concatenate([near, sides[0]], 1), jnp.concatenate([far, sides[1]], 1)]
                done = mm3(split(jnp.concatenate(lines, 0)), table)
                for i in range(slots):
                    for part, at in ((lower, 4 * EDGE * i), (upper, 4 * EDGE * i + 2 * EDGE)):
                        re, im = done[at : at + EDGE], done[at + EDGE : at + 2 * EDGE]
                        target[slots * d + i, 0:EDGE, part] = re[:, :LANES] - im[:, LANES:]
                        target[slots * d + i, EDGE:, part] = im[:, :LANES] + re[:, LANES:]
                return carry

            lax.fori_loop(first // slots, end // slots, step, 0)
    final = held[0]
    for i in range(slots):
        value = final[slots * REACH + i]
        out_ref[i] = jnp.where(i < count_ref[0], value, jnp.zeros_like(value))


def shifted(block, axis, distance):
    devices = range(lax.axis_size(axis))
    route = [((i - distance) % len(devices), i) for i in devices]
    return lax.ppermute(block, axis, route)


def call(kernel, outs, specs, scratch=()):
    return pl.pallas_call(
        kernel,
        out_shape=[jax.ShapeDtypeStruct(shape, dtype) for shape, dtype in outs],
        in_specs=specs,
        out_specs=[VMEM] * len(outs),
        scratch_shapes=list(scratch),
        compiler_params=PARAMS,
    )


def exchange(block, axis):
    parts = lax.axis_size(axis)
    shape = (parts, block.shape[0] // parts, block.shape[1])
    return lax.all_to_all(block.reshape(shape), axis, split_axis=0, concat_axis=0, tiled=True).reshape(block.shape)


def shards(base, fine_psi, counts, neighbors, base_cell):
    wide = lax.axis_size("wide")
    narrow = lax.axis_size("narrow")
    w_at = lax.axis_index("wide")
    n_at = lax.axis_index("narrow")
    _, rows_here, cols_here, length = base.shape
    slots = fine_psi.shape[0]
    chunk = length // narrow
    per = wide // narrow
    used = rows_here * chunk
    place = jnp.stack([w_at, n_at]).astype(jnp.int32)

    row = lax.all_gather(fine_psi.reshape(slots, 2 * EDGE, CELLS), "narrow", axis=0, tiled=False)
    before = shifted(row[narrow - REACH :], "wide", 1)
    after = shifted(row[:REACH], "wide", -1)

    kr, ki = circulant(length)
    (sent,) = call(
        lambda *refs: along_last(rows_here, cols_here, narrow, *refs),
        [((narrow * (cols_here + 8), LANES), F32)],
        [VMEM] * 3,
    )(base.reshape(2 * rows_here * cols_here, length), neighbors, jnp.asarray(stacked(kr, ki)))
    first = exchange(sent, "narrow")

    full = np.stack([np.stack([kr, -ki]), np.stack([ki, kr])])
    second = full.transpose(0, 2, 1, 3).reshape(2, wide, rows_here, 2 * length).transpose(0, 2, 1, 3)
    second = stacked(second.reshape(2 * length, 2 * length))
    (sent,) = call(
        lambda *refs: along_second(rows_here, chunk, wide, narrow, *refs), [((wide * 4, LANES), F32)], [VMEM] * 2
    )(first, jnp.asarray(second))
    groups = base_cell.shape[0]
    cells = jnp.transpose(base_cell, (2, 1, 0)).reshape(18, groups)
    faces = groups // LANES * 8
    data, upto, count = call(
        lambda *refs: plan(rows_here, chunk, wide, *refs),
        [((faces, 5 * LANES), BF16), ((faces, LANES), F32), ((8, LANES), jnp.int32)],
        [SMEM, VMEM],
    )(place, cells)

    got = exchange(sent, "wide")
    third = full.reshape(2, 2, wide, rows_here, wide, rows_here).transpose(0, 3, 2, 1, 5, 4)
    third = third.reshape(2 * length, 2 * rows_here, wide)
    main = third[:, :4].transpose(0, 2, 1).reshape(2 * length, 4 * wide)
    third = stacked(np.concatenate([main, third[:, 4:].reshape(2 * length, 2 * wide)], 1))
    (sent,) = call(
        lambda *refs: along_first(rows_here, chunk, wide, narrow, slots, *refs),
        [((wide * 16, LANES), F32)],
        [SMEM] + [VMEM] * 5,
        [pltpu.VMEM((16, groups + 2 * LANES), F32)],
    )(count, data, upto, first, got, jnp.asarray(third))
    got = exchange(sent, "wide")
    sent, near = call(
        lambda *refs: forward_rows(slots, wide, narrow, *refs),
        [((narrow * (4 * per + 16), LANES), F32), ((24, LANES), jnp.int32)],
        [SMEM, VMEM],
    )(place, got)
    got = exchange(sent, "narrow")
    (drifted,) = call(
        lambda *refs: unpack(rows_here, chunk, per, narrow, *refs),
        [((2 * rows_here * cols_here, length), F32)],
        [VMEM],
        [pltpu.VMEM((2 * rows_here * cols_here, LANES), F32)] * 2,
    )(got)

    total = 2 * REACH + 1
    (fine,) = call(
        lambda *refs: sweeps(slots, narrow, per, used, *refs),
        [((slots, 2 * EDGE, CELLS), F32)],
        [SMEM] * 3 + [VMEM] * 5,
        [
            pltpu.VMEM((total * slots, 2 * EDGE, CELLS), F32),
            pltpu.VMEM((total * slots, 2 * EDGE, CELLS), F32),
            pltpu.VMEM((16, LANES), F32),
            pltpu.SMEM((16, LANES), F32),
            pltpu.SemaphoreType.DMA,
        ],
    )(place, counts, near, got, before, row, after, jnp.asarray(sweep_tables()))
    return (drifted.reshape(base.shape), fine.reshape(fine_psi.shape))


def solution(mesh):
    in_specs = (
        P(None, "wide", "narrow", None),
        P(("wide", "narrow"), None, None, None),
        P(("wide", "narrow")),
        P(("wide", "narrow"), None),
        P(),
    )
    out_specs = (P(None, "wide", "narrow", None), P(("wide", "narrow"), None, None, None))
    return jax.shard_map(shards, mesh=mesh, in_specs=in_specs, out_specs=out_specs, check_vma=False)
```

```python
import jax
import jax.numpy as jnp
import ml_dtypes
import numpy as np
from jax import lax
from jax.experimental import pallas as pl
from jax.experimental.pallas import tpu as pltpu
from jax.sharding import PartitionSpec as P

SUBCYCLES = 2
PHASE_RATE = 8.0
TAYLOR_STEP = 0.6
EDGE = 16
CELLS = EDGE * EDGE
LANES = 128
ROOM = 64
REACH = 6
VMEM = pl.BlockSpec(memory_space=pltpu.VMEM)
SMEM = pl.BlockSpec(memory_space=pltpu.SMEM)
PARAMS = pltpu.CompilerParams(vmem_limit_bytes=48 * 2**20)
F32 = jnp.float32
BF16 = jnp.bfloat16


def two_parts(matrix):
    high = matrix.astype(ml_dtypes.bfloat16)
    low = (matrix - high.astype(np.float64)).astype(ml_dtypes.bfloat16)
    return high, low


def circulant(length):
    signed = np.fft.fftfreq(length, 1.0 / length)
    phase = np.exp(-1j * PHASE_RATE * (2.0 * np.pi * signed / length) ** 2)
    kernel = np.fft.ifft(phase)
    index = np.arange(length)
    matrix = kernel[(index[:, None] - index[None, :]) % length]
    return matrix.real, matrix.imag


def stacked(*matrices):
    return np.concatenate([part for m in matrices for part in two_parts(m)], 0)


def sweep_tables():
    laplace = -2.0 * np.eye(24) + np.eye(24, k=1) + np.eye(24, k=-1)
    squared = laplace @ laplace
    c = TAYLOR_STEP
    real = np.eye(24) - c**2 / 2.0 * squared + c**4 / 24.0 * squared @ squared
    imag = c * laplace - c**3 / 6.0 * squared @ laplace
    own, ghost, half = [], [], []
    for rows in (real[4:20], imag[4:20]):
        assert np.allclose(rows[:8, :16], rows[8:, 8:])
        edge = np.zeros((EDGE, EDGE))
        edge[:, 12:] = rows[:, :4]
        edge[:, :4] = rows[:, 20:]
        own.append(rows[:, 4:20])
        ghost.append(edge)
        half.append(np.concatenate([rows[:8, 4:16], rows[:8, :4]], 1))
    left = [np.block([[t[0], -t[1]], [t[1], t[0]]]) for t in (own, ghost)]
    high, low = two_parts(np.concatenate(left, 1))
    pad = np.zeros((2 * EDGE, CELLS - 12 * EDGE), high.dtype)
    left = np.concatenate([high, high, low, pad], 1)
    middle = np.concatenate([np.kron(t.T, np.eye(EDGE)) for t in half], 1)
    last = np.block([[np.kron(np.eye(8), t[i].T) for i in range(2)] for t in (own, ghost)])
    return np.concatenate([stacked(middle, last), left], 0)


def split(values):
    high = values.astype(BF16)
    return high, (values - high.astype(F32)).astype(BF16)


def halves(table_ref, index):
    size = table_ref.shape[1]
    start = 2 * size * index
    return table_ref[start : start + size, :], table_ref[start + size : start + 2 * size, :]


def mm(a, b):
    return jnp.dot(a, b, preferred_element_type=F32)


def mm3(a, b):
    return mm(a[0], b[0]) + (mm(a[1], b[0]) + mm(a[0], b[1]))


def packed(tiles):
    used = tiles[0].shape[1]
    room = LANES - used
    pad = jnp.zeros((tiles[0].shape[0], 2 * room - used), tiles[0].dtype)
    extra = [t[:, :room] for t in tiles[4:]] + [jnp.concatenate([t[:, room:], pad], 1) for t in tiles[4:]]
    return [jnp.concatenate([t, e], 1) for t, e in zip(tiles[:4], extra, strict=True)]


def unpacked(rows, used):
    room = LANES - used
    extra = [jnp.concatenate([rows[i][:, used:], rows[2 + i][:, used : 2 * used - room]], 1) for i in range(2)]
    return [t[:, :used] for t in rows] + extra


def along_last(rows_here, cols_here, parts, base_ref, near_ref, table_ref, out_ref):
    plane = rows_here * cols_here
    x = split(base_ref[...])
    pr = mm3(x, halves(table_ref, 0))
    pi = mm3(x, halves(table_ref, 1))
    done = (pr[:plane] - pi[plane:], pi[:plane] + pr[plane:])
    chunk = done[0].shape[1] // parts
    near = near_ref[...].astype(F32)
    near = jnp.concatenate([near, jnp.zeros((8 - near.shape[0], near.shape[1]), F32)], 0)
    free = LANES - cols_here // 8 * chunk
    near = jnp.concatenate([near, jnp.zeros((8, free - near.shape[1]), F32)], 1)
    pad = jnp.zeros((cols_here, LANES - (2 * rows_here - 1) * chunk), F32)
    for n in range(parts):
        pieces = [
            done[p][cols_here * x : cols_here * (x + 1), chunk * n : chunk * (n + 1)]
            for p in range(2)
            for x in range(rows_here)
        ]
        at = (cols_here + 8) * n
        out_ref[at : at + cols_here, :] = jnp.concatenate(pieces[:-1] + [pad], 1)
        last = [pieces[-1][8 * i : 8 * i + 8] for i in range(cols_here // 8)]
        out_ref[at + cols_here : at + cols_here + 8, :] = jnp.concatenate(last + [near], 1)


def along_second(rows_here, chunk, wide, narrow, x_ref, table_ref, out_ref):
    cols_here = x_ref.shape[0] // narrow - 8
    used = rows_here * chunk
    real = [x_ref[(cols_here + 8) * n : (cols_here + 8) * n + cols_here, :] for n in range(narrow)]
    real = jnp.concatenate(real, 0)
    last = []
    for n in range(narrow):
        tile = x_ref[(cols_here + 8) * n + cols_here : (cols_here + 8) * (n + 1), :]
        last += [tile[:, chunk * i : chunk * (i + 1)] for i in range(cols_here // 8)]
    last = jnp.concatenate(last, 0)
    pad = jnp.zeros((last.shape[0], LANES - used), F32)
    imag = jnp.concatenate([real[:, used : 2 * used - chunk], last, pad], 1)
    done = mm3(halves(table_ref, 0), split(jnp.concatenate([real, imag], 0)))
    tiles = []
    for p in range(2):
        for x in range(rows_here):
            pieces = [
                done[(p * rows_here + j) * wide : (p * rows_here + j + 1) * wide, chunk * x : chunk * (x + 1)]
                for j in range(rows_here)
            ]
            tiles.append(jnp.concatenate(pieces, 1))
    for q, row in enumerate(packed(tiles)):
        out_ref[pl.ds(q, wide, stride=4), :] = row


def plan(rows_here, chunk, wide, place_ref, cell_ref, data_ref, upto_ref, count_ref):
    groups = cell_ref.shape[1]
    first = cell_ref[0:6, :]
    second = cell_ref[6:12, :] - place_ref[0] * rows_here
    last = cell_ref[12:18, :] - place_ref[1] * chunk
    mine = (second >= 0) & (second < rows_here) & (last >= 0) & (last < chunk)
    owner = first // rows_here
    lane = jnp.where(mine, second * chunk + last, -1).astype(F32)
    line = ((first - owner * rows_here) * wide + owner).astype(F32)
    pad = jnp.full((2, LANES), -1.0, F32)

    def chunks(values):
        parts = [values[:, LANES * c : LANES * (c + 1)] for c in range(groups // LANES)]
        return jnp.concatenate([t for part in parts for t in (part, pad)], 0)

    lane, line = chunks(lane), chunks(line)
    mark = jnp.where(lane >= 0, 1.0, 0.0)
    rows, size = mark.shape
    earlier = lax.broadcasted_iota(jnp.int32, (size, size), 0) <= lax.broadcasted_iota(jnp.int32, (size, size), 1)
    above = lax.broadcasted_iota(jnp.int32, (rows, rows), 1) <= lax.broadcasted_iota(jnp.int32, (rows, rows), 0)
    in_row = mm(mark.astype(BF16), jnp.where(earlier, 1.0, 0.0).astype(BF16))
    in_all = jnp.broadcast_to(jnp.sum(mark, axis=1, keepdims=True), mark.shape)
    upto = mm(jnp.where(above, 1.0, 0.0).astype(BF16), in_all.astype(BF16))
    high, low = split(upto - in_all + in_row)
    upto_ref[...] = upto
    count_ref[...] = upto[rows - 8 :].astype(jnp.int32)
    data_ref[...] = jnp.concatenate([high, low] + [t.astype(BF16) for t in (mark, line, lane)], 1)


def along_first(
    rows_here, chunk, wide, narrow, slots, count_ref, data_ref, upto_ref, first_ref, x_ref, table_ref, out_ref, v_ref
):
    used = rows_here * chunk
    lines = rows_here * wide
    faces = upto_ref.shape[0]
    groups = faces // 8 * LANES
    rows = [x_ref[pl.ds(q, wide, stride=4), :] for q in range(4)]
    blank = jnp.zeros((wide, LANES - used), F32)
    extra = [jnp.concatenate([t, blank], 1) for t in unpacked(rows, used)[4:]]
    done = mm3(halves(table_ref, 0), split(jnp.concatenate([x_ref[...]] + extra, 0)))
    parts = [split(done[p * lines : (p + 1) * lines]) for p in range(2)]
    source = jnp.concatenate([parts[p][i] for i in range(2) for p in range(2)], 1)
    v_ref[...] = jnp.zeros_like(v_ref[...])
    shape = (LANES, LANES)
    row_at = lax.broadcasted_iota(jnp.int32, (faces, LANES), 0)
    deep = lax.broadcasted_iota(jnp.int32, (2 * faces, LANES), 0)
    sub = lax.broadcasted_iota(jnp.int32, shape, 0)
    lane_at = lax.broadcasted_iota(jnp.int32, shape, 1)
    line_at = lax.broadcasted_iota(jnp.int32, (LANES, lines), 1)

    def body(k, carry):
        wanted = (lane_at[:1] + k * LANES).astype(F32)
        row = jnp.sum(jnp.where(upto_ref[...] <= wanted, 1, 0), axis=0, keepdims=True)
        hot = jnp.where(row_at == row, 1.0, 0.0).T.astype(BF16)
        near = mm(hot, data_ref[...])
        rank, mark, line, lane = near[:, :LANES] + near[:, LANES : 2 * LANES], *jnp.split(near[:, 2 * LANES :], 3, 1)
        hit = jnp.where((rank == (sub + k * LANES + 1).astype(F32)) & (mark > 0.5), 1.0, 0.0)
        line = jnp.sum(hit * line, axis=1, keepdims=True).astype(jnp.int32)
        lane = jnp.sum(hit * lane, axis=1, keepdims=True).astype(jnp.int32)
        taken = mm(jnp.where(line_at == line, 1.0, 0.0).astype(BF16), source)
        back = []
        for p in range(2):
            both = taken[:, LANES * p : LANES * (p + 1)] + taken[:, LANES * (p + 2) : LANES * (p + 3)]
            back.append(jnp.sum(jnp.where(lane_at == lane, both, 0.0), axis=1, keepdims=True) * hit)
        high, low = split(jnp.concatenate(back, 0))
        goal = row // 8 * 16 + row % 8 + 4
        spread = jnp.concatenate([jnp.where(deep == goal + 6 * p, 1.0, 0.0).astype(BF16) for p in range(2)], 1)
        values = mm(spread, high) + mm(spread, low)
        for c in range(faces // 8):
            v_ref[:, LANES * (c + 1) : LANES * (c + 2)] += values[16 * c : 16 * (c + 1)]
        return carry

    lax.fori_loop(0, (count_ref[7, 0] + LANES - 1) // LANES, body, 0)
    v_ref[:, :LANES] = v_ref[:, groups : groups + LANES]
    v_ref[:, groups + LANES :] = v_ref[:, LANES : 2 * LANES]
    per_row = narrow * slots
    window = per_row + 10 * slots
    block = first_ref.shape[0] // narrow
    near = [
        first_ref[block * n + block - 8 : block * (n + 1), (block - 8) // 8 * chunk : (block - 8) // 8 * chunk + 6]
        for n in range(narrow)
    ]
    near = jnp.concatenate([t[:slots] for t in near], 1)
    near = jnp.concatenate([near, jnp.zeros((slots, LANES - window - near.shape[1]), F32)], 1)
    near = jnp.concatenate([jnp.zeros((4, LANES - window), F32), near, jnp.zeros((8, LANES - window), F32)], 0)
    for w in range(wide):
        start = LANES + w * per_row - 5 * slots
        out_ref[16 * w : 16 * w + 16, :] = jnp.concatenate([v_ref[:, start : start + window], near], 1)
    tiles = [done[wide * r : wide * (r + 1), :used] for r in range(2 * rows_here)]
    for q, row in enumerate(packed(tiles)):
        out_ref[pl.ds(q, wide, stride=16), :] = row


def forward_rows(slots, wide, narrow, used, place_ref, x_ref, out_ref, near_ref):
    per = wide // narrow
    block = 4 * per + 16
    low = jnp.zeros((8, LANES), F32)
    top = jnp.zeros((8, LANES), F32)
    for w in range(0, wide, 2):
        one = x_ref[16 * w : 16 * w + 8, :]
        two = x_ref[16 * w + 16 : 16 * w + 24, :]
        low += one + two
        top += x_ref[16 * w + 8 : 16 * w + 16, :] + x_ref[16 * w + 24 : 16 * w + 32, :]
        row = w // per * block + 4 * (w % per)
        out_ref[row : row + 8, :] = jnp.concatenate([one[:4], two[:4]], 0)
    for n in range(narrow):
        row = n * block + 4 * per
        out_ref[row : row + 8, :] = low
        out_ref[row + 8 : row + 16, :] = top
    devices = wide * narrow
    mine = place_ref[0] * narrow + place_ref[1]
    tiles = []
    for o in range(3):
        at = lax.rem(place_ref[0] + (o - 1 + wide), wide) * 16
        tiles.append(x_ref[pl.ds(pl.multiple_of(at, 16), 8), used : used + 6 * narrow])
    tiles.append(jnp.zeros((8, 2 * LANES - 18 * narrow), F32))
    numbers = jnp.concatenate(tiles, 1).astype(jnp.int32)
    owner = jnp.maximum(numbers, 0) // slots
    away = owner - mine + REACH
    away = jnp.where(away < 0, away + devices, away)
    away = jnp.where(away >= devices, away - devices, away)
    known = (numbers >= 0) & (away <= 2 * REACH)
    near = jnp.where(known, (away - owner) * slots + numbers, -1)
    shift = 2 * LANES - 6 * (place_ref[1] + narrow - REACH)
    near_ref[...] = pltpu.roll(near, shift, 1)[:, :LANES]


def needs(slots, count_ref, near_ref, list_ref, flag_ref):
    total = (2 * REACH + 1) * slots
    steps = 3 * SUBCYCLES

    def clear(i, carry):
        flag_ref[i] = 0
        return carry

    lax.fori_loop(0, (steps + 1) * ROOM, clear, 0, unroll=8)
    for i in range(slots):
        flag_ref[steps * ROOM + slots * REACH + i] = jnp.where(i < count_ref[0], 1, 0)
    for s in reversed(range(steps)):
        k = s % 3
        base, before, after = 3 * ROOM * s, ROOM * s, ROOM * (s + 1)

        def step(d, found, k=k, base=base, before=before, after=after):
            for i in range(slots):
                q = slots * d + i
                need = flag_ref[after + q]
                sides = [near_ref[4 + i, 6 * d + 2 * k + j] for j in range(2)]
                list_ref[base + found] = q
                list_ref[base + ROOM + found] = sides[0]
                list_ref[base + 2 * ROOM + found] = sides[1]
                flag_ref[before + jnp.where(need > 0, q, total)] = 1
                for side in sides:
                    flag_ref[before + jnp.where((need > 0) & (side >= 0), side, total)] = 1
                found += need
            return found

        found = lax.fori_loop(s + 1, 2 * REACH - s, step, jnp.int32(0))
        for i in range(slots):
            for j in range(3):
                list_ref[base + ROOM * j + found + i] = total
        list_ref[3 * ROOM * steps + s] = found


def unpack(rows_here, chunk, per, narrow, x_ref, out_ref, lo_ref, hi_ref):
    block = 4 * per + 16
    cols = per * rows_here
    length = out_ref.shape[1]
    tiles = [
        unpacked([x_ref[pl.ds(n * block + q, per, stride=4), :] for q in range(4)], rows_here * chunk)
        for n in range(narrow)
    ]
    for r in range(2 * rows_here):
        for y in range(rows_here):
            pieces = [t[r][:, chunk * y : chunk * (y + 1)] for t in tiles]
            line = jnp.concatenate(pieces + [jnp.zeros((per, 2 * LANES - length), F32)], 1)
            lo_ref[pl.ds(r * cols + y, per, stride=rows_here), :] = line[:, :LANES]
            hi_ref[pl.ds(r * cols + y, per, stride=rows_here), :] = line[:, LANES:]
    out_ref[:, :LANES] = lo_ref[...]
    out_ref[:, LANES:] = hi_ref[:, : length - LANES]


def sweeps(
    slots, narrow, per, used, place_ref, count_ref, list_ref, recv_ref, before_ref, row_ref, after_ref,
    table_ref, out_ref, one_ref, two_ref, edge_ref, edge_smem, sem,
):
    block = 4 * per + 16
    low = jnp.zeros((8, LANES), F32)
    top = jnp.zeros((8, LANES), F32)
    for n in range(narrow):
        row = n * block + 4 * per
        low += recv_ref[row : row + 8, :]
        top += recv_ref[row + 8 : row + 16, :]
    edge_ref[0:8, :] = low
    edge_ref[8:16, :] = top
    copy = pltpu.make_async_copy(edge_ref, edge_smem, sem)
    copy.start()
    mine = place_ref[1]
    total = 2 * REACH + 1
    for r in range(total):
        at = mine + r + narrow - REACH

        @pl.when(at < narrow)
        def _(r=r, at=at):
            one_ref[slots * r : slots * (r + 1)] = before_ref[at - (narrow - REACH)]

        @pl.when((at >= narrow) & (at < 2 * narrow))
        def _(r=r, at=at):
            one_ref[slots * r : slots * (r + 1)] = row_ref[at - narrow]

        @pl.when(at >= 2 * narrow)
        def _(r=r, at=at):
            one_ref[slots * r : slots * (r + 1)] = after_ref[at - 2 * narrow]

    copy.wait()
    row = lax.broadcasted_iota(jnp.int32, (2 * EDGE, CELLS), 0)
    real = row < EDGE
    late_row = row % EDGE >= 8
    column = lax.broadcasted_iota(jnp.int32, (2 * EDGE, LANES), 1)
    real_half = real[:, :LANES]
    early_half = column < LANES // 2
    late_last = column % EDGE >= 8
    left = table_ref[4 * CELLS :, : 12 * EDGE]
    held = [one_ref, two_ref]
    for s in range(3 * SUBCYCLES):
        k = s % 3
        source, target = held[s % 2], held[1 - s % 2]
        base = 3 * ROOM * s
        rounds = (list_ref[3 * ROOM * 3 * SUBCYCLES + s] + slots - 1) // slots

        def ghost(e, q, side, part, is_real, k=k, base=base, source=source):
            near = list_ref[base + ROOM * (1 + side) + e]
            lane = q + slots * (mine - 1)
            face = 4 + 2 * k + side
            flat = jnp.where(is_real, edge_smem[face, lane], edge_smem[6 + face, lane])
            return jnp.where(near >= 0, source[jnp.maximum(near, 0), :, part], flat)

        if k == 0:

            def step(d, carry, base=base, source=source, target=target, ghost=ghost):
                every = slice(0, CELLS)
                for i in range(slots):
                    e = slots * d + i
                    q = list_ref[base + e]
                    around = jnp.where(late_row, ghost(e, q, 0, every, real), ghost(e, q, 1, every, real))
                    high, rest = split(jnp.concatenate([source[q], around], 0))
                    target[q] = mm(left, jnp.concatenate([high, rest, high], 0))
                return carry

        else:
            table = halves(table_ref, k - 1)

            def step(d, carry, k=k, base=base, source=source, target=target, ghost=ghost, table=table):
                lower, upper = slice(0, LANES), slice(LANES, CELLS)
                lines, goals = [], []
                for i in range(slots):
                    e = slots * d + i
                    q = list_ref[base + e]
                    goals.append(q)
                    near, far = source[q, :, lower], source[q, :, upper]
                    if k == 1:
                        before = ghost(e, q, 0, upper, real_half)
                        after = ghost(e, q, 1, lower, real_half)
                        sides = jnp.where(early_half, far, before), jnp.where(early_half, after, near)
                    else:
                        sides = [
                            jnp.where(late_last, ghost(e, q, 0, part, real_half), ghost(e, q, 1, part, real_half))
                            for part in (lower, upper)
                        ]
                    lines += [jnp.concatenate([near, sides[0]], 1), jnp.concatenate([far, sides[1]], 1)]
                done = mm3(split(jnp.concatenate(lines, 0)), table)
                for i, q in enumerate(goals):
                    for part, at in ((lower, 4 * EDGE * i), (upper, 4 * EDGE * i + 2 * EDGE)):
                        re, im = done[at : at + EDGE], done[at + EDGE : at + 2 * EDGE]
                        target[q, 0:EDGE, part] = re[:, :LANES] - im[:, LANES:]
                        target[q, EDGE:, part] = im[:, :LANES] + re[:, LANES:]
                return carry

        lax.fori_loop(0, rounds, step, 0)
    final = held[0]
    for i in range(slots):
        value = final[slots * REACH + i]
        out_ref[i] = jnp.where(i < count_ref[0], value, jnp.zeros_like(value))


def shifted(block, axis, distance):
    devices = range(lax.axis_size(axis))
    route = [((i - distance) % len(devices), i) for i in devices]
    return lax.ppermute(block, axis, route)


def call(kernel, outs, specs, scratch=()):
    return pl.pallas_call(
        kernel,
        out_shape=[jax.ShapeDtypeStruct(shape, dtype) for shape, dtype in outs],
        in_specs=specs,
        out_specs=[VMEM] * len(outs),
        scratch_shapes=list(scratch),
        compiler_params=PARAMS,
    )


def exchange(block, axis):
    parts = lax.axis_size(axis)
    shape = (parts, block.shape[0] // parts, block.shape[1])
    return lax.all_to_all(block.reshape(shape), axis, split_axis=0, concat_axis=0, tiled=True).reshape(block.shape)


def shards(base, fine_psi, counts, neighbors, base_cell):
    wide = lax.axis_size("wide")
    narrow = lax.axis_size("narrow")
    w_at = lax.axis_index("wide")
    n_at = lax.axis_index("narrow")
    _, rows_here, cols_here, length = base.shape
    slots = fine_psi.shape[0]
    chunk = length // narrow
    per = wide // narrow
    used = rows_here * chunk
    place = jnp.stack([w_at, n_at]).astype(jnp.int32)

    row = lax.all_gather(fine_psi.reshape(slots, 2 * EDGE, CELLS), "narrow", axis=0, tiled=False)
    before = shifted(row[narrow - REACH :], "wide", 1)
    after = shifted(row[:REACH], "wide", -1)

    kr, ki = circulant(length)
    (sent,) = call(
        lambda *refs: along_last(rows_here, cols_here, narrow, *refs),
        [((narrow * (cols_here + 8), LANES), F32)],
        [VMEM] * 3,
    )(base.reshape(2 * rows_here * cols_here, length), neighbors, jnp.asarray(stacked(kr, ki)))
    first = exchange(sent, "narrow")

    full = np.stack([np.stack([kr, -ki]), np.stack([ki, kr])])
    second = full.transpose(0, 2, 1, 3).reshape(2, wide, rows_here, 2 * length).transpose(0, 2, 1, 3)
    second = stacked(second.reshape(2 * length, 2 * length))
    (sent,) = call(
        lambda *refs: along_second(rows_here, chunk, wide, narrow, *refs), [((wide * 4, LANES), F32)], [VMEM] * 2
    )(first, jnp.asarray(second))
    groups = base_cell.shape[0]
    cells = jnp.transpose(base_cell, (2, 1, 0)).reshape(18, groups)
    faces = groups // LANES * 8
    data, upto, count = call(
        lambda *refs: plan(rows_here, chunk, wide, *refs),
        [((faces, 5 * LANES), BF16), ((faces, LANES), F32), ((8, LANES), jnp.int32)],
        [SMEM, VMEM],
    )(place, cells)

    got = exchange(sent, "wide")
    third = full.reshape(2, 2, wide, rows_here, wide, rows_here).transpose(0, 3, 2, 1, 5, 4)
    third = third.reshape(2 * length, 2 * rows_here, wide)
    main = third[:, :4].transpose(0, 2, 1).reshape(2 * length, 4 * wide)
    third = stacked(np.concatenate([main, third[:, 4:].reshape(2 * length, 2 * wide)], 1))
    (sent,) = call(
        lambda *refs: along_first(rows_here, chunk, wide, narrow, slots, *refs),
        [((wide * 16, LANES), F32)],
        [SMEM] + [VMEM] * 5,
        [pltpu.VMEM((16, groups + 2 * LANES), F32)],
    )(count, data, upto, first, got, jnp.asarray(third))
    got = exchange(sent, "wide")
    sent, near = call(
        lambda *refs: forward_rows(slots, wide, narrow, used, *refs),
        [((narrow * (4 * per + 16), LANES), F32), ((8, LANES), jnp.int32)],
        [SMEM, VMEM],
    )(place, got)
    got = exchange(sent, "narrow")
    (drifted,) = call(
        lambda *refs: unpack(rows_here, chunk, per, narrow, *refs),
        [((2 * rows_here * cols_here, length), F32)],
        [VMEM],
        [pltpu.VMEM((2 * rows_here * cols_here, LANES), F32)] * 2,
    )(got)

    total = 2 * REACH + 1
    entries = 3 * SUBCYCLES * 3 * ROOM + LANES
    lists = pl.pallas_call(
        lambda *refs: needs(slots, *refs),
        out_shape=jax.ShapeDtypeStruct((entries,), jnp.int32),
        in_specs=[SMEM] * 2,
        out_specs=SMEM,
        scratch_shapes=[pltpu.SMEM(((3 * SUBCYCLES + 1) * ROOM,), jnp.int32)],
        compiler_params=PARAMS,
    )(counts, near)
    (fine,) = call(
        lambda *refs: sweeps(slots, narrow, per, used, *refs),
        [((slots, 2 * EDGE, CELLS), F32)],
        [SMEM] * 3 + [VMEM] * 5,
        [
            pltpu.VMEM((total * slots + 1, 2 * EDGE, CELLS), F32),
            pltpu.VMEM((total * slots + 1, 2 * EDGE, CELLS), F32),
            pltpu.VMEM((16, LANES), F32),
            pltpu.SMEM((16, LANES), F32),
            pltpu.SemaphoreType.DMA,
        ],
    )(place, counts, lists, got, before, row, after, jnp.asarray(sweep_tables()))
    return (drifted.reshape(base.shape), fine.reshape(fine_psi.shape))


def solution(mesh):
    in_specs = (
        P(None, "wide", "narrow", None),
        P(("wide", "narrow"), None, None, None),
        P(("wide", "narrow")),
        P(("wide", "narrow"), None),
        P(),
    )
    out_specs = (P(None, "wide", "narrow", None), P(("wide", "narrow"), None, None, None))
    return jax.shard_map(shards, mesh=mesh, in_specs=in_specs, out_specs=out_specs, check_vma=False)
```

```python
import jax
import jax.numpy as jnp
import ml_dtypes
import numpy as np
from jax import lax
from jax.experimental import pallas as pl
from jax.experimental.pallas import tpu as pltpu
from jax.sharding import PartitionSpec as P

SUBCYCLES = 2
PHASE_RATE = 8.0
TAYLOR_STEP = 0.6
EDGE = 16
CELLS = EDGE * EDGE
LANES = 128
ROOM = 64
REACH = 6
VMEM = pl.BlockSpec(memory_space=pltpu.VMEM)
SMEM = pl.BlockSpec(memory_space=pltpu.SMEM)
PARAMS = pltpu.CompilerParams(vmem_limit_bytes=20 * 2**20)
F32 = jnp.float32
BF16 = jnp.bfloat16


def two_parts(matrix):
    high = matrix.astype(ml_dtypes.bfloat16)
    low = (matrix - high.astype(np.float64)).astype(ml_dtypes.bfloat16)
    return high, low


def circulant(length):
    signed = np.fft.fftfreq(length, 1.0 / length)
    phase = np.exp(-1j * PHASE_RATE * (2.0 * np.pi * signed / length) ** 2)
    kernel = np.fft.ifft(phase)
    index = np.arange(length)
    matrix = kernel[(index[:, None] - index[None, :]) % length]
    return matrix.real, matrix.imag


def stacked(*matrices):
    return np.concatenate([part for m in matrices for part in two_parts(m)], 0)


def sweep_tables():
    laplace = -2.0 * np.eye(24) + np.eye(24, k=1) + np.eye(24, k=-1)
    squared = laplace @ laplace
    c = TAYLOR_STEP
    real = np.eye(24) - c**2 / 2.0 * squared + c**4 / 24.0 * squared @ squared
    imag = c * laplace - c**3 / 6.0 * squared @ laplace
    own, ghost, half = [], [], []
    for rows in (real[4:20], imag[4:20]):
        assert np.allclose(rows[:8, :16], rows[8:, 8:])
        edge = np.zeros((EDGE, EDGE))
        edge[:, 12:] = rows[:, :4]
        edge[:, :4] = rows[:, 20:]
        own.append(rows[:, 4:20])
        ghost.append(edge)
        half.append(np.concatenate([rows[:8, 4:16], rows[:8, :4]], 1))
    left = [np.block([[t[0], -t[1]], [t[1], t[0]]]) for t in (own, ghost)]
    high, low = two_parts(np.concatenate(left, 1))
    pad = np.zeros((2 * EDGE, CELLS - 12 * EDGE), high.dtype)
    left = np.concatenate([high, high, low, pad], 1)
    middle = np.concatenate([np.kron(t.T, np.eye(EDGE)) for t in half], 1)
    last = np.block([[np.kron(np.eye(8), t[i].T) for i in range(2)] for t in (own, ghost)])
    return np.concatenate([stacked(middle, last), left], 0)


def split(values):
    high = values.astype(BF16)
    return high, (values - high.astype(F32)).astype(BF16)


def halves(table_ref, index):
    size = table_ref.shape[1]
    start = 2 * size * index
    return table_ref[start : start + size, :], table_ref[start + size : start + 2 * size, :]


def mm(a, b):
    return jnp.dot(a, b, preferred_element_type=F32)


def mm3(a, b):
    return mm(a[0], b[0]) + (mm(a[1], b[0]) + mm(a[0], b[1]))


def packed(tiles):
    used = tiles[0].shape[1]
    room = LANES - used
    pad = jnp.zeros((tiles[0].shape[0], 2 * room - used), tiles[0].dtype)
    extra = [t[:, :room] for t in tiles[4:]] + [jnp.concatenate([t[:, room:], pad], 1) for t in tiles[4:]]
    return [jnp.concatenate([t, e], 1) for t, e in zip(tiles[:4], extra, strict=True)]


def unpacked(rows, used):
    room = LANES - used
    extra = [jnp.concatenate([rows[i][:, used:], rows[2 + i][:, used : 2 * used - room]], 1) for i in range(2)]
    return [t[:, :used] for t in rows] + extra


def along_last(rows_here, cols_here, parts, base_ref, near_ref, table_ref, out_ref):
    plane = rows_here * cols_here
    x = split(base_ref[...])
    pr = mm3(x, halves(table_ref, 0))
    pi = mm3(x, halves(table_ref, 1))
    done = (pr[:plane] - pi[plane:], pi[:plane] + pr[plane:])
    chunk = done[0].shape[1] // parts
    near = near_ref[...].astype(F32)
    near = jnp.concatenate([near, jnp.zeros((8 - near.shape[0], near.shape[1]), F32)], 0)
    free = LANES - cols_here // 8 * chunk
    near = jnp.concatenate([near, jnp.zeros((8, free - near.shape[1]), F32)], 1)
    pad = jnp.zeros((cols_here, LANES - (2 * rows_here - 1) * chunk), F32)
    for n in range(parts):
        pieces = [
            done[p][cols_here * x : cols_here * (x + 1), chunk * n : chunk * (n + 1)]
            for p in range(2)
            for x in range(rows_here)
        ]
        at = (cols_here + 8) * n
        out_ref[at : at + cols_here, :] = jnp.concatenate(pieces[:-1] + [pad], 1)
        last = [pieces[-1][8 * i : 8 * i + 8] for i in range(cols_here // 8)]
        out_ref[at + cols_here : at + cols_here + 8, :] = jnp.concatenate(last + [near], 1)


def along_second(rows_here, chunk, wide, narrow, x_ref, table_ref, out_ref):
    cols_here = x_ref.shape[0] // narrow - 8
    used = rows_here * chunk
    real = [x_ref[(cols_here + 8) * n : (cols_here + 8) * n + cols_here, :] for n in range(narrow)]
    real = jnp.concatenate(real, 0)
    last = []
    for n in range(narrow):
        tile = x_ref[(cols_here + 8) * n + cols_here : (cols_here + 8) * (n + 1), :]
        last += [tile[:, chunk * i : chunk * (i + 1)] for i in range(cols_here // 8)]
    last = jnp.concatenate(last, 0)
    pad = jnp.zeros((last.shape[0], LANES - used), F32)
    imag = jnp.concatenate([real[:, used : 2 * used - chunk], last, pad], 1)
    done = mm3(halves(table_ref, 0), split(jnp.concatenate([real, imag], 0)))
    tiles = []
    for p in range(2):
        for x in range(rows_here):
            pieces = [
                done[(p * rows_here + j) * wide : (p * rows_here + j + 1) * wide, chunk * x : chunk * (x + 1)]
                for j in range(rows_here)
            ]
            tiles.append(jnp.concatenate(pieces, 1))
    for q, row in enumerate(packed(tiles)):
        out_ref[pl.ds(q, wide, stride=4), :] = row


def plan(rows_here, chunk, wide, place_ref, cell_ref, data_ref, upto_ref, count_ref):
    groups = cell_ref.shape[1]
    first = cell_ref[0:6, :]
    second = cell_ref[6:12, :] - place_ref[0] * rows_here
    last = cell_ref[12:18, :] - place_ref[1] * chunk
    mine = (second >= 0) & (second < rows_here) & (last >= 0) & (last < chunk)
    owner = first // rows_here
    lane = jnp.where(mine, second * chunk + last, -1).astype(F32)
    line = ((first - owner * rows_here) * wide + owner).astype(F32)
    pad = jnp.full((2, LANES), -1.0, F32)

    def chunks(values):
        parts = [values[:, LANES * c : LANES * (c + 1)] for c in range(groups // LANES)]
        return jnp.concatenate([t for part in parts for t in (part, pad)], 0)

    lane, line = chunks(lane), chunks(line)
    mark = jnp.where(lane >= 0, 1.0, 0.0)
    rows, size = mark.shape
    earlier = lax.broadcasted_iota(jnp.int32, (size, size), 0) <= lax.broadcasted_iota(jnp.int32, (size, size), 1)
    above = lax.broadcasted_iota(jnp.int32, (rows, rows), 1) <= lax.broadcasted_iota(jnp.int32, (rows, rows), 0)
    in_row = mm(mark.astype(BF16), jnp.where(earlier, 1.0, 0.0).astype(BF16))
    in_all = jnp.broadcast_to(jnp.sum(mark, axis=1, keepdims=True), mark.shape)
    upto = mm(jnp.where(above, 1.0, 0.0).astype(BF16), in_all.astype(BF16))
    high, low = split(upto - in_all + in_row)
    upto_ref[...] = upto
    count_ref[...] = upto[rows - 8 :].astype(jnp.int32)
    data_ref[...] = jnp.concatenate([high, low] + [t.astype(BF16) for t in (mark, line, lane)], 1)


def along_first(
    rows_here, chunk, wide, narrow, slots, count_ref, data_ref, upto_ref, first_ref, x_ref, table_ref, out_ref, v_ref
):
    used = rows_here * chunk
    lines = rows_here * wide
    faces = upto_ref.shape[0]
    groups = faces // 8 * LANES
    rows = [x_ref[pl.ds(q, wide, stride=4), :] for q in range(4)]
    blank = jnp.zeros((wide, LANES - used), F32)
    extra = [jnp.concatenate([t, blank], 1) for t in unpacked(rows, used)[4:]]
    done = mm3(halves(table_ref, 0), split(jnp.concatenate([x_ref[...]] + extra, 0)))
    parts = [split(done[p * lines : (p + 1) * lines]) for p in range(2)]
    source = jnp.concatenate([parts[p][i] for i in range(2) for p in range(2)], 1)
    v_ref[...] = jnp.zeros_like(v_ref[...])
    shape = (LANES, LANES)
    row_at = lax.broadcasted_iota(jnp.int32, (faces, LANES), 0)
    deep = lax.broadcasted_iota(jnp.int32, (2 * faces, LANES), 0)
    sub = lax.broadcasted_iota(jnp.int32, shape, 0)
    lane_at = lax.broadcasted_iota(jnp.int32, shape, 1)
    line_at = lax.broadcasted_iota(jnp.int32, (LANES, lines), 1)

    def body(k, carry):
        wanted = (lane_at[:1] + k * LANES).astype(F32)
        row = jnp.sum(jnp.where(upto_ref[...] <= wanted, 1, 0), axis=0, keepdims=True)
        hot = jnp.where(row_at == row, 1.0, 0.0).T.astype(BF16)
        near = mm(hot, data_ref[...])
        rank, mark, line, lane = near[:, :LANES] + near[:, LANES : 2 * LANES], *jnp.split(near[:, 2 * LANES :], 3, 1)
        hit = jnp.where((rank == (sub + k * LANES + 1).astype(F32)) & (mark > 0.5), 1.0, 0.0)
        line = jnp.sum(hit * line, axis=1, keepdims=True).astype(jnp.int32)
        lane = jnp.sum(hit * lane, axis=1, keepdims=True).astype(jnp.int32)
        taken = mm(jnp.where(line_at == line, 1.0, 0.0).astype(BF16), source)
        back = []
        for p in range(2):
            both = taken[:, LANES * p : LANES * (p + 1)] + taken[:, LANES * (p + 2) : LANES * (p + 3)]
            back.append(jnp.sum(jnp.where(lane_at == lane, both, 0.0), axis=1, keepdims=True) * hit)
        high, low = split(jnp.concatenate(back, 0))
        goal = row // 8 * 16 + row % 8 + 4
        spread = jnp.concatenate([jnp.where(deep == goal + 6 * p, 1.0, 0.0).astype(BF16) for p in range(2)], 1)
        values = mm(spread, high) + mm(spread, low)
        for c in range(faces // 8):
            v_ref[:, LANES * (c + 1) : LANES * (c + 2)] += values[16 * c : 16 * (c + 1)]
        return carry

    lax.fori_loop(0, (count_ref[7, 0] + LANES - 1) // LANES, body, 0)
    v_ref[:, :LANES] = v_ref[:, groups : groups + LANES]
    v_ref[:, groups + LANES :] = v_ref[:, LANES : 2 * LANES]
    per_row = narrow * slots
    window = per_row + 10 * slots
    block = first_ref.shape[0] // narrow
    near = [
        first_ref[block * n + block - 8 : block * (n + 1), (block - 8) // 8 * chunk : (block - 8) // 8 * chunk + 6]
        for n in range(narrow)
    ]
    near = jnp.concatenate([t[:slots] for t in near], 1)
    near = jnp.concatenate([near, jnp.zeros((slots, LANES - window - near.shape[1]), F32)], 1)
    near = jnp.concatenate([jnp.zeros((4, LANES - window), F32), near, jnp.zeros((8, LANES - window), F32)], 0)
    for w in range(wide):
        start = LANES + w * per_row - 5 * slots
        out_ref[16 * w : 16 * w + 16, :] = jnp.concatenate([v_ref[:, start : start + window], near], 1)
    tiles = [done[wide * r : wide * (r + 1), :used] for r in range(2 * rows_here)]
    for q, row in enumerate(packed(tiles)):
        out_ref[pl.ds(q, wide, stride=16), :] = row


def forward_rows(slots, wide, narrow, used, place_ref, x_ref, out_ref, near_ref):
    per = wide // narrow
    block = 4 * per + 16
    low = jnp.zeros((8, LANES), F32)
    top = jnp.zeros((8, LANES), F32)
    for w in range(0, wide, 2):
        one = x_ref[16 * w : 16 * w + 8, :]
        two = x_ref[16 * w + 16 : 16 * w + 24, :]
        low += one + two
        top += x_ref[16 * w + 8 : 16 * w + 16, :] + x_ref[16 * w + 24 : 16 * w + 32, :]
        row = w // per * block + 4 * (w % per)
        out_ref[row : row + 8, :] = jnp.concatenate([one[:4], two[:4]], 0)
    for n in range(narrow):
        row = n * block + 4 * per
        out_ref[row : row + 8, :] = low
        out_ref[row + 8 : row + 16, :] = top
    devices = wide * narrow
    mine = place_ref[0] * narrow + place_ref[1]
    tiles = []
    for o in range(3):
        at = lax.rem(place_ref[0] + (o - 1 + wide), wide) * 16
        tiles.append(x_ref[pl.ds(pl.multiple_of(at, 16), 8), used : used + 6 * narrow])
    tiles.append(jnp.zeros((8, 2 * LANES - 18 * narrow), F32))
    numbers = jnp.concatenate(tiles, 1).astype(jnp.int32)
    owner = jnp.maximum(numbers, 0) // slots
    away = owner - mine + REACH
    away = jnp.where(away < 0, away + devices, away)
    away = jnp.where(away >= devices, away - devices, away)
    known = (numbers >= 0) & (away <= 2 * REACH)
    near = jnp.where(known, (away - owner) * slots + numbers, -1)
    shift = 2 * LANES - 6 * (place_ref[1] + narrow - REACH)
    near_ref[...] = pltpu.roll(near, shift, 1)[:, :LANES]


def needs(slots, count_ref, near_ref, list_ref, flag_ref):
    total = (2 * REACH + 1) * slots
    steps = 3 * SUBCYCLES

    def clear(i, carry):
        flag_ref[i] = 0
        return carry

    lax.fori_loop(0, (steps + 1) * ROOM, clear, 0, unroll=8)
    for i in range(slots):
        flag_ref[steps * ROOM + slots * REACH + i] = jnp.where(i < count_ref[0], 1, 0)
    for s in reversed(range(steps)):
        k = s % 3
        base, before, after = 3 * ROOM * s, ROOM * s, ROOM * (s + 1)

        def step(d, found, k=k, base=base, before=before, after=after):
            for i in range(slots):
                q = slots * d + i
                need = flag_ref[after + q]
                sides = [near_ref[4 + i, 6 * d + 2 * k + j] for j in range(2)]
                list_ref[base + found] = q
                list_ref[base + ROOM + found] = sides[0]
                list_ref[base + 2 * ROOM + found] = sides[1]
                flag_ref[before + jnp.where(need > 0, q, total)] = 1
                for side in sides:
                    flag_ref[before + jnp.where((need > 0) & (side >= 0), side, total)] = 1
                found += need
            return found

        found = lax.fori_loop(s + 1, 2 * REACH - s, step, jnp.int32(0))
        for i in range(slots):
            for j in range(3):
                list_ref[base + ROOM * j + found + i] = total
        list_ref[3 * ROOM * steps + s] = found


def unpack(rows_here, chunk, per, narrow, x_ref, out_ref, lo_ref, hi_ref):
    block = 4 * per + 16
    cols = per * rows_here
    length = out_ref.shape[1]
    tiles = [
        unpacked([x_ref[pl.ds(n * block + q, per, stride=4), :] for q in range(4)], rows_here * chunk)
        for n in range(narrow)
    ]
    for r in range(2 * rows_here):
        for y in range(rows_here):
            pieces = [t[r][:, chunk * y : chunk * (y + 1)] for t in tiles]
            line = jnp.concatenate(pieces + [jnp.zeros((per, 2 * LANES - length), F32)], 1)
            lo_ref[pl.ds(r * cols + y, per, stride=rows_here), :] = line[:, :LANES]
            hi_ref[pl.ds(r * cols + y, per, stride=rows_here), :] = line[:, LANES:]
    out_ref[:, :LANES] = lo_ref[...]
    out_ref[:, LANES:] = hi_ref[:, : length - LANES]


def sweeps(
    slots, narrow, per, used, place_ref, count_ref, list_ref, recv_ref, before_ref, row_ref, after_ref,
    table_ref, out_ref, one_ref, two_ref, edge_ref, edge_smem, sem,
):
    block = 4 * per + 16
    low = jnp.zeros((8, LANES), F32)
    top = jnp.zeros((8, LANES), F32)
    for n in range(narrow):
        row = n * block + 4 * per
        low += recv_ref[row : row + 8, :]
        top += recv_ref[row + 8 : row + 16, :]
    edge_ref[0:8, :] = low
    edge_ref[8:16, :] = top
    copy = pltpu.make_async_copy(edge_ref, edge_smem, sem)
    copy.start()
    mine = place_ref[1]
    total = 2 * REACH + 1
    for r in range(total):
        at = mine + r + narrow - REACH
        place = (r - REACH + 4) % narrow

        @pl.when(at < narrow)
        def _(r=r, place=place):
            one_ref[slots * r : slots * (r + 1)] = before_ref[place]

        @pl.when((at >= narrow) & (at < 2 * narrow))
        def _(r=r, place=place):
            one_ref[slots * r : slots * (r + 1)] = row_ref[place]

        @pl.when(at >= 2 * narrow)
        def _(r=r, place=place):
            one_ref[slots * r : slots * (r + 1)] = after_ref[place]

    copy.wait()
    row = lax.broadcasted_iota(jnp.int32, (2 * EDGE, CELLS), 0)
    real = row < EDGE
    late_row = row % EDGE >= 8
    column = lax.broadcasted_iota(jnp.int32, (2 * EDGE, LANES), 1)
    real_half = real[:, :LANES]
    early_half = column < LANES // 2
    late_last = column % EDGE >= 8
    left = table_ref[4 * CELLS :, : 12 * EDGE]
    held = [one_ref, two_ref]
    for s in range(3 * SUBCYCLES):
        k = s % 3
        source, target = held[s % 2], held[1 - s % 2]
        base = 3 * ROOM * s
        rounds = (list_ref[3 * ROOM * 3 * SUBCYCLES + s] + slots - 1) // slots

        def ghost(e, q, side, part, is_real, k=k, base=base, source=source):
            near = list_ref[base + ROOM * (1 + side) + e]
            lane = q + slots * (mine - 1)
            face = 4 + 2 * k + side
            flat = jnp.where(is_real, edge_smem[face, lane], edge_smem[6 + face, lane])
            return jnp.where(near >= 0, source[jnp.maximum(near, 0), :, part], flat)

        if k == 0:

            def step(d, carry, base=base, source=source, target=target, ghost=ghost):
                every = slice(0, CELLS)
                for i in range(slots):
                    e = slots * d + i
                    q = list_ref[base + e]
                    around = jnp.where(late_row, ghost(e, q, 0, every, real), ghost(e, q, 1, every, real))
                    high, rest = split(jnp.concatenate([source[q], around], 0))
                    target[q] = mm(left, jnp.concatenate([high, rest, high], 0))
                return carry

        else:
            table = halves(table_ref, k - 1)

            def step(d, carry, k=k, base=base, source=source, target=target, ghost=ghost, table=table):
                lower, upper = slice(0, LANES), slice(LANES, CELLS)
                lines, goals = [], []
                for i in range(slots):
                    e = slots * d + i
                    q = list_ref[base + e]
                    goals.append(q)
                    near, far = source[q, :, lower], source[q, :, upper]
                    if k == 1:
                        before = ghost(e, q, 0, upper, real_half)
                        after = ghost(e, q, 1, lower, real_half)
                        sides = jnp.where(early_half, far, before), jnp.where(early_half, after, near)
                    else:
                        sides = [
                            jnp.where(late_last, ghost(e, q, 0, part, real_half), ghost(e, q, 1, part, real_half))
                            for part in (lower, upper)
                        ]
                    lines += [jnp.concatenate([near, sides[0]], 1), jnp.concatenate([far, sides[1]], 1)]
                done = mm3(split(jnp.concatenate(lines, 0)), table)
                for i, q in enumerate(goals):
                    for part, at in ((lower, 4 * EDGE * i), (upper, 4 * EDGE * i + 2 * EDGE)):
                        re, im = done[at : at + EDGE], done[at + EDGE : at + 2 * EDGE]
                        target[q, 0:EDGE, part] = re[:, :LANES] - im[:, LANES:]
                        target[q, EDGE:, part] = im[:, :LANES] + re[:, LANES:]
                return carry

        lax.fori_loop(0, rounds, step, 0)
    final = held[0]
    for i in range(slots):
        value = final[slots * REACH + i]
        out_ref[i] = jnp.where(i < count_ref[0], value, jnp.zeros_like(value))


def shifted(block, axis, distance):
    devices = range(lax.axis_size(axis))
    route = [((i - distance) % len(devices), i) for i in devices]
    return lax.ppermute(block, axis, route)


def call(kernel, outs, specs, scratch=()):
    return pl.pallas_call(
        kernel,
        out_shape=[jax.ShapeDtypeStruct(shape, dtype) for shape, dtype in outs],
        in_specs=specs,
        out_specs=[VMEM] * len(outs),
        scratch_shapes=list(scratch),
        compiler_params=PARAMS,
    )


def exchange(block, axis):
    parts = lax.axis_size(axis)
    shape = (parts, block.shape[0] // parts, block.shape[1])
    return lax.all_to_all(block.reshape(shape), axis, split_axis=0, concat_axis=0, tiled=True).reshape(block.shape)


def shards(base, fine_psi, counts, neighbors, base_cell):
    wide = lax.axis_size("wide")
    narrow = lax.axis_size("narrow")
    w_at = lax.axis_index("wide")
    n_at = lax.axis_index("narrow")
    _, rows_here, cols_here, length = base.shape
    slots = fine_psi.shape[0]
    chunk = length // narrow
    per = wide // narrow
    used = rows_here * chunk
    place = jnp.stack([w_at, n_at]).astype(jnp.int32)

    patches = fine_psi.reshape(1, slots, 2 * EDGE, CELLS)
    trio = jnp.concatenate([shifted(patches, "narrow", 1), patches, shifted(patches, "narrow", -1)], 0)
    row = jnp.concatenate([shifted(trio, "narrow", 3), trio, shifted(trio[:2], "narrow", -3)], 0)
    before = shifted(row, "wide", 1)
    after = shifted(row, "wide", -1)

    kr, ki = circulant(length)
    (sent,) = call(
        lambda *refs: along_last(rows_here, cols_here, narrow, *refs),
        [((narrow * (cols_here + 8), LANES), F32)],
        [VMEM] * 3,
    )(base.reshape(2 * rows_here * cols_here, length), neighbors, jnp.asarray(stacked(kr, ki)))
    first = exchange(sent, "narrow")

    full = np.stack([np.stack([kr, -ki]), np.stack([ki, kr])])
    second = full.transpose(0, 2, 1, 3).reshape(2, wide, rows_here, 2 * length).transpose(0, 2, 1, 3)
    second = stacked(second.reshape(2 * length, 2 * length))
    (sent,) = call(
        lambda *refs: along_second(rows_here, chunk, wide, narrow, *refs), [((wide * 4, LANES), F32)], [VMEM] * 2
    )(first, jnp.asarray(second))
    groups = base_cell.shape[0]
    cells = jnp.transpose(base_cell, (2, 1, 0)).reshape(18, groups)
    faces = groups // LANES * 8
    data, upto, count = call(
        lambda *refs: plan(rows_here, chunk, wide, *refs),
        [((faces, 5 * LANES), BF16), ((faces, LANES), F32), ((8, LANES), jnp.int32)],
        [SMEM, VMEM],
    )(place, cells)

    got = exchange(sent, "wide")
    third = full.reshape(2, 2, wide, rows_here, wide, rows_here).transpose(0, 3, 2, 1, 5, 4)
    third = third.reshape(2 * length, 2 * rows_here, wide)
    main = third[:, :4].transpose(0, 2, 1).reshape(2 * length, 4 * wide)
    third = stacked(np.concatenate([main, third[:, 4:].reshape(2 * length, 2 * wide)], 1))
    (sent,) = call(
        lambda *refs: along_first(rows_here, chunk, wide, narrow, slots, *refs),
        [((wide * 16, LANES), F32)],
        [SMEM] + [VMEM] * 5,
        [pltpu.VMEM((16, groups + 2 * LANES), F32)],
    )(count, data, upto, first, got, jnp.asarray(third))
    got = exchange(sent, "wide")
    sent, near = call(
        lambda *refs: forward_rows(slots, wide, narrow, used, *refs),
        [((narrow * (4 * per + 16), LANES), F32), ((8, LANES), jnp.int32)],
        [SMEM, VMEM],
    )(place, got)
    got = exchange(sent, "narrow")
    (drifted,) = call(
        lambda *refs: unpack(rows_here, chunk, per, narrow, *refs),
        [((2 * rows_here * cols_here, length), F32)],
        [VMEM],
        [pltpu.VMEM((2 * rows_here * cols_here, LANES), F32)] * 2,
    )(got)

    total = 2 * REACH + 1
    entries = 3 * SUBCYCLES * 3 * ROOM + LANES
    lists = pl.pallas_call(
        lambda *refs: needs(slots, *refs),
        out_shape=jax.ShapeDtypeStruct((entries,), jnp.int32),
        in_specs=[SMEM] * 2,
        out_specs=SMEM,
        scratch_shapes=[pltpu.SMEM(((3 * SUBCYCLES + 1) * ROOM,), jnp.int32)],
        compiler_params=PARAMS,
    )(counts, near)
    (fine,) = call(
        lambda *refs: sweeps(slots, narrow, per, used, *refs),
        [((slots, 2 * EDGE, CELLS), F32)],
        [SMEM] * 3 + [VMEM] * 5,
        [
            pltpu.VMEM((total * slots + 1, 2 * EDGE, CELLS), F32),
            pltpu.VMEM((total * slots + 1, 2 * EDGE, CELLS), F32),
            pltpu.VMEM((16, LANES), F32),
            pltpu.SMEM((16, LANES), F32),
            pltpu.SemaphoreType.DMA,
        ],
    )(place, counts, lists, got, before, row, after, jnp.asarray(sweep_tables()))
    return (drifted.reshape(base.shape), fine.reshape(fine_psi.shape))


def solution(mesh):
    in_specs = (
        P(None, "wide", "narrow", None),
        P(("wide", "narrow"), None, None, None),
        P(("wide", "narrow")),
        P(("wide", "narrow"), None),
        P(),
    )
    out_specs = (P(None, "wide", "narrow", None), P(("wide", "narrow"), None, None, None))
    return jax.shard_map(shards, mesh=mesh, in_specs=in_specs, out_specs=out_specs, check_vma=False)
```

```python
import jax
import jax.numpy as jnp
import ml_dtypes
import numpy as np
from jax import lax
from jax.experimental import pallas as pl
from jax.experimental.pallas import tpu as pltpu
from jax.sharding import PartitionSpec as P

SUBCYCLES = 2
PHASE_RATE = 8.0
TAYLOR_STEP = 0.6
EDGE = 16
CELLS = EDGE * EDGE
LANES = 128
ROOM = 64
REACH = 6
VMEM = pl.BlockSpec(memory_space=pltpu.VMEM)
SMEM = pl.BlockSpec(memory_space=pltpu.SMEM)
PARAMS = pltpu.CompilerParams(vmem_limit_bytes=20 * 2**20)
WHOLE = pltpu.CompilerParams(vmem_limit_bytes=60 * 2**20)
F32 = jnp.float32
BF16 = jnp.bfloat16


def two_parts(matrix):
    high = matrix.astype(ml_dtypes.bfloat16)
    low = (matrix - high.astype(np.float64)).astype(ml_dtypes.bfloat16)
    return high, low


def circulant(length):
    signed = np.fft.fftfreq(length, 1.0 / length)
    phase = np.exp(-1j * PHASE_RATE * (2.0 * np.pi * signed / length) ** 2)
    kernel = np.fft.ifft(phase)
    index = np.arange(length)
    matrix = kernel[(index[:, None] - index[None, :]) % length]
    return matrix.real, matrix.imag


def stacked(*matrices):
    return np.concatenate([part for m in matrices for part in two_parts(m)], 0)


def sweep_tables():
    laplace = -2.0 * np.eye(24) + np.eye(24, k=1) + np.eye(24, k=-1)
    squared = laplace @ laplace
    c = TAYLOR_STEP
    real = np.eye(24) - c**2 / 2.0 * squared + c**4 / 24.0 * squared @ squared
    imag = c * laplace - c**3 / 6.0 * squared @ laplace
    own, ghost, half = [], [], []
    for rows in (real[4:20], imag[4:20]):
        assert np.allclose(rows[:8, :16], rows[8:, 8:])
        edge = np.zeros((EDGE, EDGE))
        edge[:, 12:] = rows[:, :4]
        edge[:, :4] = rows[:, 20:]
        own.append(rows[:, 4:20])
        ghost.append(edge)
        half.append(np.concatenate([rows[:8, 4:16], rows[:8, :4]], 1))
    left = [np.block([[t[0], -t[1]], [t[1], t[0]]]) for t in (own, ghost)]
    high, low = two_parts(np.concatenate(left, 1))
    pad = np.zeros((2 * EDGE, CELLS - 12 * EDGE), high.dtype)
    left = np.concatenate([high, high, low, pad], 1)
    middle = np.concatenate([np.kron(t.T, np.eye(EDGE)) for t in half], 1)
    last = np.block([[np.kron(np.eye(8), t[i].T) for i in range(2)] for t in (own, ghost)])
    return np.concatenate([stacked(middle, last), left], 0)


def split(values):
    high = values.astype(BF16)
    return high, (values - high.astype(F32)).astype(BF16)


def halves(table_ref, index):
    size = table_ref.shape[1]
    start = 2 * size * index
    return table_ref[start : start + size, :], table_ref[start + size : start + 2 * size, :]


def mm(a, b):
    return jnp.dot(a, b, preferred_element_type=F32)


def mm3(a, b):
    return mm(a[0], b[0]) + (mm(a[1], b[0]) + mm(a[0], b[1]))


def packed(tiles):
    used = tiles[0].shape[1]
    room = LANES - used
    pad = jnp.zeros((tiles[0].shape[0], 2 * room - used), tiles[0].dtype)
    extra = [t[:, :room] for t in tiles[4:]] + [jnp.concatenate([t[:, room:], pad], 1) for t in tiles[4:]]
    return [jnp.concatenate([t, e], 1) for t, e in zip(tiles[:4], extra, strict=True)]


def unpacked(rows, used):
    room = LANES - used
    extra = [jnp.concatenate([rows[i][:, used:], rows[2 + i][:, used : 2 * used - room]], 1) for i in range(2)]
    return [t[:, :used] for t in rows] + extra


def along_last(rows_here, cols_here, parts, base_hbm, near_hbm, table_hbm, out_ref, base_ref, near_ref, table_ref, sems):
    pairs = ((base_hbm, base_ref), (near_hbm, near_ref), (table_hbm, table_ref))
    copies = [pltpu.make_async_copy(a, b, sems.at[i]) for i, (a, b) in enumerate(pairs)]
    for copy in copies:
        copy.start()
    for copy in copies:
        copy.wait()
    plane = rows_here * cols_here
    x = split(base_ref[...])
    pr = mm3(x, halves(table_ref, 0))
    pi = mm3(x, halves(table_ref, 1))
    done = (pr[:plane] - pi[plane:], pi[:plane] + pr[plane:])
    chunk = done[0].shape[1] // parts
    near = near_ref[...].astype(F32)
    near = jnp.concatenate([near, jnp.zeros((8 - near.shape[0], near.shape[1]), F32)], 0)
    free = LANES - cols_here // 8 * chunk
    near = jnp.concatenate([near, jnp.zeros((8, free - near.shape[1]), F32)], 1)
    pad = jnp.zeros((cols_here, LANES - (2 * rows_here - 1) * chunk), F32)
    for n in range(parts):
        pieces = [
            done[p][cols_here * x : cols_here * (x + 1), chunk * n : chunk * (n + 1)]
            for p in range(2)
            for x in range(rows_here)
        ]
        at = (cols_here + 8) * n
        out_ref[at : at + cols_here, :] = jnp.concatenate(pieces[:-1] + [pad], 1)
        last = [pieces[-1][8 * i : 8 * i + 8] for i in range(cols_here // 8)]
        out_ref[at + cols_here : at + cols_here + 8, :] = jnp.concatenate(last + [near], 1)


def along_second(rows_here, chunk, wide, narrow, x_ref, table_ref, out_ref):
    cols_here = x_ref.shape[0] // narrow - 8
    used = rows_here * chunk
    real = [x_ref[(cols_here + 8) * n : (cols_here + 8) * n + cols_here, :] for n in range(narrow)]
    real = jnp.concatenate(real, 0)
    last = []
    for n in range(narrow):
        tile = x_ref[(cols_here + 8) * n + cols_here : (cols_here + 8) * (n + 1), :]
        last += [tile[:, chunk * i : chunk * (i + 1)] for i in range(cols_here // 8)]
    last = jnp.concatenate(last, 0)
    pad = jnp.zeros((last.shape[0], LANES - used), F32)
    imag = jnp.concatenate([real[:, used : 2 * used - chunk], last, pad], 1)
    done = mm3(halves(table_ref, 0), split(jnp.concatenate([real, imag], 0)))
    tiles = []
    for p in range(2):
        for x in range(rows_here):
            pieces = [
                done[(p * rows_here + j) * wide : (p * rows_here + j + 1) * wide, chunk * x : chunk * (x + 1)]
                for j in range(rows_here)
            ]
            tiles.append(jnp.concatenate(pieces, 1))
    for q, row in enumerate(packed(tiles)):
        out_ref[pl.ds(q, wide, stride=4), :] = row


def plan(rows_here, chunk, wide, place_ref, cell_ref, data_ref, upto_ref, count_ref):
    groups = cell_ref.shape[1]
    first = cell_ref[0:6, :]
    second = cell_ref[6:12, :] - place_ref[0] * rows_here
    last = cell_ref[12:18, :] - place_ref[1] * chunk
    mine = (second >= 0) & (second < rows_here) & (last >= 0) & (last < chunk)
    owner = first // rows_here
    lane = jnp.where(mine, second * chunk + last, -1).astype(F32)
    line = ((first - owner * rows_here) * wide + owner).astype(F32)
    pad = jnp.full((2, LANES), -1.0, F32)

    def chunks(values):
        parts = [values[:, LANES * c : LANES * (c + 1)] for c in range(groups // LANES)]
        return jnp.concatenate([t for part in parts for t in (part, pad)], 0)

    lane, line = chunks(lane), chunks(line)
    mark = jnp.where(lane >= 0, 1.0, 0.0)
    rows, size = mark.shape
    earlier = lax.broadcasted_iota(jnp.int32, (size, size), 0) <= lax.broadcasted_iota(jnp.int32, (size, size), 1)
    above = lax.broadcasted_iota(jnp.int32, (rows, rows), 1) <= lax.broadcasted_iota(jnp.int32, (rows, rows), 0)
    in_row = mm(mark.astype(BF16), jnp.where(earlier, 1.0, 0.0).astype(BF16))
    in_all = jnp.broadcast_to(jnp.sum(mark, axis=1, keepdims=True), mark.shape)
    upto = mm(jnp.where(above, 1.0, 0.0).astype(BF16), in_all.astype(BF16))
    high, low = split(upto - in_all + in_row)
    upto_ref[...] = upto
    count_ref[...] = upto[rows - 8 :].astype(jnp.int32)
    data_ref[...] = jnp.concatenate([high, low] + [t.astype(BF16) for t in (mark, line, lane)], 1)


def along_first(
    rows_here, chunk, wide, narrow, slots, count_ref, data_ref, upto_ref, first_ref, x_ref, table_ref, out_ref, v_ref
):
    used = rows_here * chunk
    lines = rows_here * wide
    faces = upto_ref.shape[0]
    groups = faces // 8 * LANES
    rows = [x_ref[pl.ds(q, wide, stride=4), :] for q in range(4)]
    blank = jnp.zeros((wide, LANES - used), F32)
    extra = [jnp.concatenate([t, blank], 1) for t in unpacked(rows, used)[4:]]
    done = mm3(halves(table_ref, 0), split(jnp.concatenate([x_ref[...]] + extra, 0)))
    parts = [split(done[p * lines : (p + 1) * lines]) for p in range(2)]
    source = jnp.concatenate([parts[p][i] for i in range(2) for p in range(2)], 1)
    v_ref[...] = jnp.zeros_like(v_ref[...])
    shape = (LANES, LANES)
    row_at = lax.broadcasted_iota(jnp.int32, (faces, LANES), 0)
    deep = lax.broadcasted_iota(jnp.int32, (2 * faces, LANES), 0)
    sub = lax.broadcasted_iota(jnp.int32, shape, 0)
    lane_at = lax.broadcasted_iota(jnp.int32, shape, 1)
    line_at = lax.broadcasted_iota(jnp.int32, (LANES, lines), 1)

    def body(k, carry):
        wanted = (lane_at[:1] + k * LANES).astype(F32)
        row = jnp.sum(jnp.where(upto_ref[...] <= wanted, 1, 0), axis=0, keepdims=True)
        hot = jnp.where(row_at == row, 1.0, 0.0).T.astype(BF16)
        near = mm(hot, data_ref[...])
        rank, mark, line, lane = near[:, :LANES] + near[:, LANES : 2 * LANES], *jnp.split(near[:, 2 * LANES :], 3, 1)
        hit = jnp.where((rank == (sub + k * LANES + 1).astype(F32)) & (mark > 0.5), 1.0, 0.0)
        line = jnp.sum(hit * line, axis=1, keepdims=True).astype(jnp.int32)
        lane = jnp.sum(hit * lane, axis=1, keepdims=True).astype(jnp.int32)
        taken = mm(jnp.where(line_at == line, 1.0, 0.0).astype(BF16), source)
        back = []
        for p in range(2):
            both = taken[:, LANES * p : LANES * (p + 1)] + taken[:, LANES * (p + 2) : LANES * (p + 3)]
            back.append(jnp.sum(jnp.where(lane_at == lane, both, 0.0), axis=1, keepdims=True) * hit)
        high, low = split(jnp.concatenate(back, 0))
        goal = row // 8 * 16 + row % 8 + 4
        spread = jnp.concatenate([jnp.where(deep == goal + 6 * p, 1.0, 0.0).astype(BF16) for p in range(2)], 1)
        values = mm(spread, high) + mm(spread, low)
        for c in range(faces // 8):
            v_ref[:, LANES * (c + 1) : LANES * (c + 2)] += values[16 * c : 16 * (c + 1)]
        return carry

    lax.fori_loop(0, (count_ref[7, 0] + LANES - 1) // LANES, body, 0)
    v_ref[:, :LANES] = v_ref[:, groups : groups + LANES]
    v_ref[:, groups + LANES :] = v_ref[:, LANES : 2 * LANES]
    per_row = narrow * slots
    window = per_row + 10 * slots
    block = first_ref.shape[0] // narrow
    near = [
        first_ref[block * n + block - 8 : block * (n + 1), (block - 8) // 8 * chunk : (block - 8) // 8 * chunk + 6]
        for n in range(narrow)
    ]
    near = jnp.concatenate([t[:slots] for t in near], 1)
    near = jnp.concatenate([near, jnp.zeros((slots, LANES - window - near.shape[1]), F32)], 1)
    near = jnp.concatenate([jnp.zeros((4, LANES - window), F32), near, jnp.zeros((8, LANES - window), F32)], 0)
    for w in range(wide):
        start = LANES + w * per_row - 5 * slots
        out_ref[16 * w : 16 * w + 16, :] = jnp.concatenate([v_ref[:, start : start + window], near], 1)
    tiles = [done[wide * r : wide * (r + 1), :used] for r in range(2 * rows_here)]
    for q, row in enumerate(packed(tiles)):
        out_ref[pl.ds(q, wide, stride=16), :] = row


def forward_rows(slots, wide, narrow, used, place_ref, x_ref, out_ref, near_ref):
    per = wide // narrow
    block = 4 * per + 16
    low = jnp.zeros((8, LANES), F32)
    top = jnp.zeros((8, LANES), F32)
    for w in range(0, wide, 2):
        one = x_ref[16 * w : 16 * w + 8, :]
        two = x_ref[16 * w + 16 : 16 * w + 24, :]
        low += one + two
        top += x_ref[16 * w + 8 : 16 * w + 16, :] + x_ref[16 * w + 24 : 16 * w + 32, :]
        row = w // per * block + 4 * (w % per)
        out_ref[row : row + 8, :] = jnp.concatenate([one[:4], two[:4]], 0)
    for n in range(narrow):
        row = n * block + 4 * per
        out_ref[row : row + 8, :] = low
        out_ref[row + 8 : row + 16, :] = top
    devices = wide * narrow
    mine = place_ref[0] * narrow + place_ref[1]
    tiles = []
    for o in range(3):
        at = lax.rem(place_ref[0] + (o - 1 + wide), wide) * 16
        tiles.append(x_ref[pl.ds(pl.multiple_of(at, 16), 8), used : used + 6 * narrow])
    tiles.append(jnp.zeros((8, 2 * LANES - 18 * narrow), F32))
    numbers = jnp.concatenate(tiles, 1).astype(jnp.int32)
    owner = jnp.maximum(numbers, 0) // slots
    away = owner - mine + REACH
    away = jnp.where(away < 0, away + devices, away)
    away = jnp.where(away >= devices, away - devices, away)
    known = (numbers >= 0) & (away <= 2 * REACH)
    near = jnp.where(known, (away - owner) * slots + numbers, -1)
    shift = 2 * LANES - 6 * (place_ref[1] + narrow - REACH)
    near_ref[...] = pltpu.roll(near, shift, 1)[:, :LANES]


def needs(slots, count_ref, near_ref, list_ref, flag_ref):
    total = (2 * REACH + 1) * slots
    steps = 3 * SUBCYCLES

    def clear(i, carry):
        flag_ref[i] = 0
        return carry

    lax.fori_loop(0, (steps + 1) * ROOM, clear, 0, unroll=8)
    for i in range(slots):
        flag_ref[steps * ROOM + slots * REACH + i] = jnp.where(i < count_ref[0], 1, 0)
    for s in reversed(range(steps)):
        k = s % 3
        base, before, after = 3 * ROOM * s, ROOM * s, ROOM * (s + 1)

        def step(d, found, k=k, base=base, before=before, after=after):
            for i in range(slots):
                q = slots * d + i
                need = flag_ref[after + q]
                sides = [near_ref[4 + i, 6 * d + 2 * k + j] for j in range(2)]
                list_ref[base + found] = q
                list_ref[base + ROOM + found] = sides[0]
                list_ref[base + 2 * ROOM + found] = sides[1]
                flag_ref[before + jnp.where(need > 0, q, total)] = 1
                for side in sides:
                    flag_ref[before + jnp.where((need > 0) & (side >= 0), side, total)] = 1
                found += need
            return found

        found = lax.fori_loop(s + 1, 2 * REACH - s, step, jnp.int32(0))
        for i in range(slots):
            for j in range(3):
                list_ref[base + ROOM * j + found + i] = total
        list_ref[3 * ROOM * steps + s] = found


def unpack(rows_here, chunk, per, narrow, x_ref, out_ref, lo_ref, hi_ref):
    block = 4 * per + 16
    cols = per * rows_here
    length = out_ref.shape[1]
    tiles = [
        unpacked([x_ref[pl.ds(n * block + q, per, stride=4), :] for q in range(4)], rows_here * chunk)
        for n in range(narrow)
    ]
    for r in range(2 * rows_here):
        for y in range(rows_here):
            pieces = [t[r][:, chunk * y : chunk * (y + 1)] for t in tiles]
            line = jnp.concatenate(pieces + [jnp.zeros((per, 2 * LANES - length), F32)], 1)
            lo_ref[pl.ds(r * cols + y, per, stride=rows_here), :] = line[:, :LANES]
            hi_ref[pl.ds(r * cols + y, per, stride=rows_here), :] = line[:, LANES:]
    out_ref[:, :LANES] = lo_ref[...]
    out_ref[:, LANES:] = hi_ref[:, : length - LANES]


def sweeps(
    slots, narrow, per, used, place_ref, count_ref, list_ref, recv_ref, before_ref, row_ref, after_ref,
    table_ref, out_ref, one_ref, two_ref, edge_ref, edge_smem, sem,
):
    block = 4 * per + 16
    low = jnp.zeros((8, LANES), F32)
    top = jnp.zeros((8, LANES), F32)
    for n in range(narrow):
        row = n * block + 4 * per
        low += recv_ref[row : row + 8, :]
        top += recv_ref[row + 8 : row + 16, :]
    edge_ref[0:8, :] = low
    edge_ref[8:16, :] = top
    copy = pltpu.make_async_copy(edge_ref, edge_smem, sem)
    copy.start()
    mine = place_ref[1]
    total = 2 * REACH + 1
    for r in range(total):
        at = mine + r + narrow - REACH
        place = (r - REACH + 4) % narrow

        @pl.when(at < narrow)
        def _(r=r, place=place):
            one_ref[slots * r : slots * (r + 1)] = before_ref[place]

        @pl.when((at >= narrow) & (at < 2 * narrow))
        def _(r=r, place=place):
            one_ref[slots * r : slots * (r + 1)] = row_ref[place]

        @pl.when(at >= 2 * narrow)
        def _(r=r, place=place):
            one_ref[slots * r : slots * (r + 1)] = after_ref[place]

    copy.wait()
    row = lax.broadcasted_iota(jnp.int32, (2 * EDGE, CELLS), 0)
    real = row < EDGE
    late_row = row % EDGE >= 8
    column = lax.broadcasted_iota(jnp.int32, (2 * EDGE, LANES), 1)
    real_half = real[:, :LANES]
    early_half = column < LANES // 2
    late_last = column % EDGE >= 8
    left = table_ref[4 * CELLS :, : 12 * EDGE]
    held = [one_ref, two_ref]
    for s in range(3 * SUBCYCLES):
        k = s % 3
        source, target = held[s % 2], held[1 - s % 2]
        base = 3 * ROOM * s
        rounds = (list_ref[3 * ROOM * 3 * SUBCYCLES + s] + slots - 1) // slots

        def ghost(e, q, side, part, is_real, k=k, base=base, source=source):
            near = list_ref[base + ROOM * (1 + side) + e]
            lane = q + slots * (mine - 1)
            face = 4 + 2 * k + side
            flat = jnp.where(is_real, edge_smem[face, lane], edge_smem[6 + face, lane])
            return jnp.where(near >= 0, source[jnp.maximum(near, 0), :, part], flat)

        if k == 0:

            def step(d, carry, base=base, source=source, target=target, ghost=ghost):
                every = slice(0, CELLS)
                for i in range(slots):
                    e = slots * d + i
                    q = list_ref[base + e]
                    around = jnp.where(late_row, ghost(e, q, 0, every, real), ghost(e, q, 1, every, real))
                    high, rest = split(jnp.concatenate([source[q], around], 0))
                    target[q] = mm(left, jnp.concatenate([high, rest, high], 0))
                return carry

        else:
            table = halves(table_ref, k - 1)

            def step(d, carry, k=k, base=base, source=source, target=target, ghost=ghost, table=table):
                lower, upper = slice(0, LANES), slice(LANES, CELLS)
                lines, goals = [], []
                for i in range(slots):
                    e = slots * d + i
                    q = list_ref[base + e]
                    goals.append(q)
                    near, far = source[q, :, lower], source[q, :, upper]
                    if k == 1:
                        before = ghost(e, q, 0, upper, real_half)
                        after = ghost(e, q, 1, lower, real_half)
                        sides = jnp.where(early_half, far, before), jnp.where(early_half, after, near)
                    else:
                        sides = [
                            jnp.where(late_last, ghost(e, q, 0, part, real_half), ghost(e, q, 1, part, real_half))
                            for part in (lower, upper)
                        ]
                    lines += [jnp.concatenate([near, sides[0]], 1), jnp.concatenate([far, sides[1]], 1)]
                done = mm3(split(jnp.concatenate(lines, 0)), table)
                for i, q in enumerate(goals):
                    for part, at in ((lower, 4 * EDGE * i), (upper, 4 * EDGE * i + 2 * EDGE)):
                        re, im = done[at : at + EDGE], done[at + EDGE : at + 2 * EDGE]
                        target[q, 0:EDGE, part] = re[:, :LANES] - im[:, LANES:]
                        target[q, EDGE:, part] = im[:, :LANES] + re[:, LANES:]
                return carry

        lax.fori_loop(0, rounds, step, 0)
    final = held[0]
    for i in range(slots):
        value = final[slots * REACH + i]
        out_ref[i] = jnp.where(i < count_ref[0], value, jnp.zeros_like(value))


def shifted(block, axis, distance):
    devices = range(lax.axis_size(axis))
    route = [((i - distance) % len(devices), i) for i in devices]
    return lax.ppermute(block, axis, route)


def call(kernel, outs, specs, scratch=(), params=PARAMS):
    return pl.pallas_call(
        kernel,
        out_shape=[jax.ShapeDtypeStruct(shape, dtype) for shape, dtype in outs],
        in_specs=specs,
        out_specs=[VMEM] * len(outs),
        scratch_shapes=list(scratch),
        compiler_params=params,
    )


def exchange(block, axis):
    parts = lax.axis_size(axis)
    shape = (parts, block.shape[0] // parts, block.shape[1])
    return lax.all_to_all(block.reshape(shape), axis, split_axis=0, concat_axis=0, tiled=True).reshape(block.shape)


def shards(base, fine_psi, counts, neighbors, base_cell):
    wide = lax.axis_size("wide")
    narrow = lax.axis_size("narrow")
    w_at = lax.axis_index("wide")
    n_at = lax.axis_index("narrow")
    _, rows_here, cols_here, length = base.shape
    slots = fine_psi.shape[0]
    chunk = length // narrow
    per = wide // narrow
    used = rows_here * chunk
    place = jnp.stack([w_at, n_at]).astype(jnp.int32)

    patches = fine_psi.reshape(1, slots, 2 * EDGE, CELLS)
    trio = jnp.concatenate([shifted(patches, "narrow", 1), patches, shifted(patches, "narrow", -1)], 0)
    row = jnp.concatenate([shifted(trio, "narrow", 3), trio, shifted(trio[:2], "narrow", -3)], 0)
    before = shifted(row, "wide", 1)
    after = shifted(row, "wide", -1)

    kr, ki = circulant(length)
    (sent,) = call(
        lambda *refs: along_last(rows_here, cols_here, narrow, *refs),
        [((narrow * (cols_here + 8), LANES), F32)],
        [pl.BlockSpec(memory_space=pl.ANY)] * 3,
        [
            pltpu.VMEM((2 * rows_here * cols_here, length), F32),
            pltpu.VMEM(neighbors.shape, jnp.int32),
            pltpu.VMEM((4 * length, length), BF16),
            pltpu.SemaphoreType.DMA((3,)),
        ],
        WHOLE,
    )(base.reshape(2 * rows_here * cols_here, length), neighbors, jnp.asarray(stacked(kr, ki)))
    first = exchange(sent, "narrow")

    full = np.stack([np.stack([kr, -ki]), np.stack([ki, kr])])
    second = full.transpose(0, 2, 1, 3).reshape(2, wide, rows_here, 2 * length).transpose(0, 2, 1, 3)
    second = stacked(second.reshape(2 * length, 2 * length))
    (sent,) = call(
        lambda *refs: along_second(rows_here, chunk, wide, narrow, *refs), [((wide * 4, LANES), F32)], [VMEM] * 2
    )(first, jnp.asarray(second))
    groups = base_cell.shape[0]
    cells = jnp.transpose(base_cell, (2, 1, 0)).reshape(18, groups)
    faces = groups // LANES * 8
    data, upto, count = call(
        lambda *refs: plan(rows_here, chunk, wide, *refs),
        [((faces, 5 * LANES), BF16), ((faces, LANES), F32), ((8, LANES), jnp.int32)],
        [SMEM, VMEM],
    )(place, cells)

    got = exchange(sent, "wide")
    third = full.reshape(2, 2, wide, rows_here, wide, rows_here).transpose(0, 3, 2, 1, 5, 4)
    third = third.reshape(2 * length, 2 * rows_here, wide)
    main = third[:, :4].transpose(0, 2, 1).reshape(2 * length, 4 * wide)
    third = stacked(np.concatenate([main, third[:, 4:].reshape(2 * length, 2 * wide)], 1))
    (sent,) = call(
        lambda *refs: along_first(rows_here, chunk, wide, narrow, slots, *refs),
        [((wide * 16, LANES), F32)],
        [SMEM] + [VMEM] * 5,
        [pltpu.VMEM((16, groups + 2 * LANES), F32)],
    )(count, data, upto, first, got, jnp.asarray(third))
    got = exchange(sent, "wide")
    sent, near = call(
        lambda *refs: forward_rows(slots, wide, narrow, used, *refs),
        [((narrow * (4 * per + 16), LANES), F32), ((8, LANES), jnp.int32)],
        [SMEM, VMEM],
    )(place, got)
    got = exchange(sent, "narrow")
    (drifted,) = call(
        lambda *refs: unpack(rows_here, chunk, per, narrow, *refs),
        [((2 * rows_here * cols_here, length), F32)],
        [VMEM],
        [pltpu.VMEM((2 * rows_here * cols_here, LANES), F32)] * 2,
    )(got)

    total = 2 * REACH + 1
    entries = 3 * SUBCYCLES * 3 * ROOM + LANES
    lists = pl.pallas_call(
        lambda *refs: needs(slots, *refs),
        out_shape=jax.ShapeDtypeStruct((entries,), jnp.int32),
        in_specs=[SMEM] * 2,
        out_specs=SMEM,
        scratch_shapes=[pltpu.SMEM(((3 * SUBCYCLES + 1) * ROOM,), jnp.int32)],
        compiler_params=PARAMS,
    )(counts, near)
    (fine,) = call(
        lambda *refs: sweeps(slots, narrow, per, used, *refs),
        [((slots, 2 * EDGE, CELLS), F32)],
        [SMEM] * 3 + [VMEM] * 5,
        [
            pltpu.VMEM((total * slots + 1, 2 * EDGE, CELLS), F32),
            pltpu.VMEM((total * slots + 1, 2 * EDGE, CELLS), F32),
            pltpu.VMEM((16, LANES), F32),
            pltpu.SMEM((16, LANES), F32),
            pltpu.SemaphoreType.DMA,
        ],
    )(place, counts, lists, got, before, row, after, jnp.asarray(sweep_tables()))
    return (drifted.reshape(base.shape), fine.reshape(fine_psi.shape))


def solution(mesh):
    in_specs = (
        P(None, "wide", "narrow", None),
        P(("wide", "narrow"), None, None, None),
        P(("wide", "narrow")),
        P(("wide", "narrow"), None),
        P(),
    )
    out_specs = (P(None, "wide", "narrow", None), P(("wide", "narrow"), None, None, None))
    return jax.shard_map(shards, mesh=mesh, in_specs=in_specs, out_specs=out_specs, check_vma=False)
```

```python
import jax
import jax.numpy as jnp
import ml_dtypes
import numpy as np
from jax import lax
from jax.experimental import pallas as pl
from jax.experimental.pallas import tpu as pltpu
from jax.sharding import PartitionSpec as P

SUBCYCLES = 2
PHASE_RATE = 8.0
TAYLOR_STEP = 0.6
EDGE = 16
CELLS = EDGE * EDGE
LANES = 128
ROOM = 64
REACH = 6
VMEM = pl.BlockSpec(memory_space=pltpu.VMEM)
SMEM = pl.BlockSpec(memory_space=pltpu.SMEM)
PARAMS = pltpu.CompilerParams(vmem_limit_bytes=20 * 2**20)
WHOLE = pltpu.CompilerParams(vmem_limit_bytes=60 * 2**20)
F32 = jnp.float32
BF16 = jnp.bfloat16


def two_parts(matrix):
    high = matrix.astype(ml_dtypes.bfloat16)
    low = (matrix - high.astype(np.float64)).astype(ml_dtypes.bfloat16)
    return high, low


def circulant(length):
    signed = np.fft.fftfreq(length, 1.0 / length)
    phase = np.exp(-1j * PHASE_RATE * (2.0 * np.pi * signed / length) ** 2)
    kernel = np.fft.ifft(phase)
    index = np.arange(length)
    matrix = kernel[(index[:, None] - index[None, :]) % length]
    return matrix.real, matrix.imag


def stacked(*matrices):
    return np.concatenate([part for m in matrices for part in two_parts(m)], 0)


def sweep_tables():
    laplace = -2.0 * np.eye(24) + np.eye(24, k=1) + np.eye(24, k=-1)
    squared = laplace @ laplace
    c = TAYLOR_STEP
    real = np.eye(24) - c**2 / 2.0 * squared + c**4 / 24.0 * squared @ squared
    imag = c * laplace - c**3 / 6.0 * squared @ laplace
    own, ghost, half = [], [], []
    for rows in (real[4:20], imag[4:20]):
        assert np.allclose(rows[:8, :16], rows[8:, 8:])
        edge = np.zeros((EDGE, EDGE))
        edge[:, 12:] = rows[:, :4]
        edge[:, :4] = rows[:, 20:]
        own.append(rows[:, 4:20])
        ghost.append(edge)
        half.append(np.concatenate([rows[:8, 4:16], rows[:8, :4]], 1))
    left = [np.block([[t[0], -t[1]], [t[1], t[0]]]) for t in (own, ghost)]
    high, low = two_parts(np.concatenate(left, 1))
    pad = np.zeros((2 * EDGE, CELLS - 12 * EDGE), high.dtype)
    left = np.concatenate([high, high, low, pad], 1)
    middle = np.concatenate([np.kron(t.T, np.eye(EDGE)) for t in half], 1)
    last = np.block([[np.kron(np.eye(8), t[i].T) for i in range(2)] for t in (own, ghost)])
    return np.concatenate([stacked(middle, last), left], 0)


def split(values):
    high = values.astype(BF16)
    return high, (values - high.astype(F32)).astype(BF16)


def halves(table_ref, index):
    size = table_ref.shape[1]
    start = 2 * size * index
    return table_ref[start : start + size, :], table_ref[start + size : start + 2 * size, :]


def mm(a, b):
    return jnp.dot(a, b, preferred_element_type=F32)


def mm3(a, b):
    return mm(a[0], b[0]) + (mm(a[1], b[0]) + mm(a[0], b[1]))


def packed(tiles):
    used = tiles[0].shape[1]
    room = LANES - used
    pad = jnp.zeros((tiles[0].shape[0], 2 * room - used), tiles[0].dtype)
    extra = [t[:, :room] for t in tiles[4:]] + [jnp.concatenate([t[:, room:], pad], 1) for t in tiles[4:]]
    return [jnp.concatenate([t, e], 1) for t, e in zip(tiles[:4], extra, strict=True)]


def unpacked(rows, used):
    room = LANES - used
    extra = [jnp.concatenate([rows[i][:, used:], rows[2 + i][:, used : 2 * used - room]], 1) for i in range(2)]
    return [t[:, :used] for t in rows] + extra


def along_last(rows_here, cols_here, parts, base_hbm, near_hbm, table_hbm, out_ref, base_ref, near_ref, table_ref, sems):
    pairs = ((base_hbm, base_ref), (near_hbm, near_ref), (table_hbm, table_ref))
    copies = [pltpu.make_async_copy(a, b, sems.at[i]) for i, (a, b) in enumerate(pairs)]
    for copy in copies:
        copy.start()
    for copy in copies:
        copy.wait()
    plane = rows_here * cols_here
    x = split(base_ref[...])
    pr = mm3(x, halves(table_ref, 0))
    pi = mm3(x, halves(table_ref, 1))
    done = (pr[:plane] - pi[plane:], pi[:plane] + pr[plane:])
    chunk = done[0].shape[1] // parts
    near = near_ref[...].astype(F32)
    near = jnp.concatenate([near, jnp.zeros((8 - near.shape[0], near.shape[1]), F32)], 0)
    free = LANES - cols_here // 8 * chunk
    near = jnp.concatenate([near, jnp.zeros((8, free - near.shape[1]), F32)], 1)
    pad = jnp.zeros((cols_here, LANES - (2 * rows_here - 1) * chunk), F32)
    for n in range(parts):
        pieces = [
            done[p][cols_here * x : cols_here * (x + 1), chunk * n : chunk * (n + 1)]
            for p in range(2)
            for x in range(rows_here)
        ]
        at = (cols_here + 8) * n
        out_ref[at : at + cols_here, :] = jnp.concatenate(pieces[:-1] + [pad], 1)
        last = [pieces[-1][8 * i : 8 * i + 8] for i in range(cols_here // 8)]
        out_ref[at + cols_here : at + cols_here + 8, :] = jnp.concatenate(last + [near], 1)


def along_second(rows_here, chunk, wide, narrow, x_ref, table_ref, out_ref):
    cols_here = x_ref.shape[0] // narrow - 8
    used = rows_here * chunk
    real = [x_ref[(cols_here + 8) * n : (cols_here + 8) * n + cols_here, :] for n in range(narrow)]
    real = jnp.concatenate(real, 0)
    last = []
    for n in range(narrow):
        tile = x_ref[(cols_here + 8) * n + cols_here : (cols_here + 8) * (n + 1), :]
        last += [tile[:, chunk * i : chunk * (i + 1)] for i in range(cols_here // 8)]
    last = jnp.concatenate(last, 0)
    pad = jnp.zeros((last.shape[0], LANES - used), F32)
    imag = jnp.concatenate([real[:, used : 2 * used - chunk], last, pad], 1)
    done = mm3(halves(table_ref, 0), split(jnp.concatenate([real, imag], 0)))
    tiles = []
    for p in range(2):
        for x in range(rows_here):
            pieces = [
                done[(p * rows_here + j) * wide : (p * rows_here + j + 1) * wide, chunk * x : chunk * (x + 1)]
                for j in range(rows_here)
            ]
            tiles.append(jnp.concatenate(pieces, 1))
    for q, row in enumerate(packed(tiles)):
        out_ref[pl.ds(q, wide, stride=4), :] = row


def located(k, upto, data):
    faces = upto.shape[0]
    row_at = lax.broadcasted_iota(jnp.int32, (faces, LANES), 0)
    sub = lax.broadcasted_iota(jnp.int32, (LANES, LANES), 0)
    wanted = (lax.broadcasted_iota(jnp.int32, (1, LANES), 1) + k * LANES).astype(F32)
    row = jnp.sum(jnp.where(upto <= wanted, 1, 0), axis=0, keepdims=True)
    hot = jnp.where(row_at == row, 1.0, 0.0).T.astype(BF16)
    near = mm(hot, data)
    rank, mark, line, lane = near[:, :LANES] + near[:, LANES : 2 * LANES], *jnp.split(near[:, 2 * LANES :], 3, 1)
    hit = jnp.where((rank == (sub + k * LANES + 1).astype(F32)) & (mark > 0.5), 1.0, 0.0)
    line = jnp.sum(hit * line, axis=1, keepdims=True).astype(jnp.int32)
    lane = jnp.sum(hit * lane, axis=1, keepdims=True).astype(jnp.int32)
    return row, line, lane, hit


def plan(rows_here, chunk, wide, place_ref, cell_ref, data_ref, upto_ref, count_ref, hit_ref, at_ref, goal_ref):
    groups = cell_ref.shape[1]
    first = cell_ref[0:6, :]
    second = cell_ref[6:12, :] - place_ref[0] * rows_here
    last = cell_ref[12:18, :] - place_ref[1] * chunk
    mine = (second >= 0) & (second < rows_here) & (last >= 0) & (last < chunk)
    owner = first // rows_here
    lane = jnp.where(mine, second * chunk + last, -1).astype(F32)
    line = ((first - owner * rows_here) * wide + owner).astype(F32)
    pad = jnp.full((2, LANES), -1.0, F32)

    def chunks(values):
        parts = [values[:, LANES * c : LANES * (c + 1)] for c in range(groups // LANES)]
        return jnp.concatenate([t for part in parts for t in (part, pad)], 0)

    lane, line = chunks(lane), chunks(line)
    mark = jnp.where(lane >= 0, 1.0, 0.0)
    rows, size = mark.shape
    earlier = lax.broadcasted_iota(jnp.int32, (size, size), 0) <= lax.broadcasted_iota(jnp.int32, (size, size), 1)
    above = lax.broadcasted_iota(jnp.int32, (rows, rows), 1) <= lax.broadcasted_iota(jnp.int32, (rows, rows), 0)
    in_row = mm(mark.astype(BF16), jnp.where(earlier, 1.0, 0.0).astype(BF16))
    in_all = jnp.broadcast_to(jnp.sum(mark, axis=1, keepdims=True), mark.shape)
    upto = mm(jnp.where(above, 1.0, 0.0).astype(BF16), in_all.astype(BF16))
    high, low = split(upto - in_all + in_row)
    upto_ref[...] = upto
    count_ref[...] = upto[rows - 8 :].astype(jnp.int32)
    data = jnp.concatenate([high, low] + [t.astype(BF16) for t in (mark, line, lane)], 1)
    data_ref[...] = data
    row, line, lane, hit = located(0, upto, data)
    hit_ref[...] = hit
    at_ref[...] = jnp.concatenate([jnp.broadcast_to(t, hit.shape) for t in (line, lane)], 1)
    goal_ref[...] = jnp.broadcast_to(row, goal_ref.shape)


def along_first(
    rows_here, chunk, wide, narrow, slots, count_ref, data_ref, upto_ref, hit_ref, at_ref, goal_ref, first_ref, x_ref, table_ref, out_ref, v_ref
):
    used = rows_here * chunk
    lines = rows_here * wide
    faces = upto_ref.shape[0]
    groups = faces // 8 * LANES
    rows = [x_ref[pl.ds(q, wide, stride=4), :] for q in range(4)]
    blank = jnp.zeros((wide, LANES - used), F32)
    extra = [jnp.concatenate([t, blank], 1) for t in unpacked(rows, used)[4:]]
    done = mm3(halves(table_ref, 0), split(jnp.concatenate([x_ref[...]] + extra, 0)))
    parts = [split(done[p * lines : (p + 1) * lines]) for p in range(2)]
    source = jnp.concatenate([parts[p][i] for i in range(2) for p in range(2)], 1)
    v_ref[...] = jnp.zeros_like(v_ref[...])
    shape = (LANES, LANES)
    deep = lax.broadcasted_iota(jnp.int32, (2 * faces, LANES), 0)
    lane_at = lax.broadcasted_iota(jnp.int32, shape, 1)
    line_at = lax.broadcasted_iota(jnp.int32, (LANES, lines), 1)

    def pick(row, line, lane, hit):
        taken = mm(jnp.where(line_at == line, 1.0, 0.0).astype(BF16), source)
        back = []
        for p in range(2):
            both = taken[:, LANES * p : LANES * (p + 1)] + taken[:, LANES * (p + 2) : LANES * (p + 3)]
            back.append(jnp.sum(jnp.where(lane_at == lane, both, 0.0), axis=1, keepdims=True) * hit)
        high, low = split(jnp.concatenate(back, 0))
        goal = row // 8 * 16 + row % 8 + 4
        spread = jnp.concatenate([jnp.where(deep == goal + 6 * p, 1.0, 0.0).astype(BF16) for p in range(2)], 1)
        values = mm(spread, high) + mm(spread, low)
        for c in range(faces // 8):
            v_ref[:, LANES * (c + 1) : LANES * (c + 2)] += values[16 * c : 16 * (c + 1)]

    def body(k, carry):
        pick(*located(k, upto_ref[...], data_ref[...]))
        return carry

    pick(goal_ref[:1], at_ref[:, :1], at_ref[:, LANES : LANES + 1], hit_ref[...])
    lax.fori_loop(1, (count_ref[7, 0] + LANES - 1) // LANES, body, 0)
    v_ref[:, :LANES] = v_ref[:, groups : groups + LANES]
    v_ref[:, groups + LANES :] = v_ref[:, LANES : 2 * LANES]
    per_row = narrow * slots
    window = per_row + 10 * slots
    block = first_ref.shape[0] // narrow
    near = [
        first_ref[block * n + block - 8 : block * (n + 1), (block - 8) // 8 * chunk : (block - 8) // 8 * chunk + 6]
        for n in range(narrow)
    ]
    near = jnp.concatenate([t[:slots] for t in near], 1)
    near = jnp.concatenate([near, jnp.zeros((slots, LANES - window - near.shape[1]), F32)], 1)
    near = jnp.concatenate([jnp.zeros((4, LANES - window), F32), near, jnp.zeros((8, LANES - window), F32)], 0)
    for w in range(wide):
        start = LANES + w * per_row - 5 * slots
        out_ref[16 * w : 16 * w + 16, :] = jnp.concatenate([v_ref[:, start : start + window], near], 1)
    tiles = [done[wide * r : wide * (r + 1), :used] for r in range(2 * rows_here)]
    for q, row in enumerate(packed(tiles)):
        out_ref[pl.ds(q, wide, stride=16), :] = row


def forward_rows(slots, wide, narrow, used, place_ref, x_ref, out_ref, near_ref):
    per = wide // narrow
    block = 4 * per + 16
    low = jnp.zeros((8, LANES), F32)
    top = jnp.zeros((8, LANES), F32)
    for w in range(0, wide, 2):
        one = x_ref[16 * w : 16 * w + 8, :]
        two = x_ref[16 * w + 16 : 16 * w + 24, :]
        low += one + two
        top += x_ref[16 * w + 8 : 16 * w + 16, :] + x_ref[16 * w + 24 : 16 * w + 32, :]
        row = w // per * block + 4 * (w % per)
        out_ref[row : row + 8, :] = jnp.concatenate([one[:4], two[:4]], 0)
    for n in range(narrow):
        row = n * block + 4 * per
        out_ref[row : row + 8, :] = low
        out_ref[row + 8 : row + 16, :] = top
    devices = wide * narrow
    mine = place_ref[0] * narrow + place_ref[1]
    tiles = []
    for o in range(3):
        at = lax.rem(place_ref[0] + (o - 1 + wide), wide) * 16
        tiles.append(x_ref[pl.ds(pl.multiple_of(at, 16), 8), used : used + 6 * narrow])
    tiles.append(jnp.zeros((8, 2 * LANES - 18 * narrow), F32))
    numbers = jnp.concatenate(tiles, 1).astype(jnp.int32)
    owner = jnp.maximum(numbers, 0) // slots
    away = owner - mine + REACH
    away = jnp.where(away < 0, away + devices, away)
    away = jnp.where(away >= devices, away - devices, away)
    known = (numbers >= 0) & (away <= 2 * REACH)
    near = jnp.where(known, (away - owner) * slots + numbers, -1)
    shift = 2 * LANES - 6 * (place_ref[1] + narrow - REACH)
    near_ref[...] = pltpu.roll(near, shift, 1)[:, :LANES]


def needs(slots, count_ref, near_ref, list_ref, flag_ref):
    total = (2 * REACH + 1) * slots
    steps = 3 * SUBCYCLES

    def clear(i, carry):
        flag_ref[i] = 0
        return carry

    lax.fori_loop(0, (steps + 1) * ROOM, clear, 0, unroll=8)
    for i in range(slots):
        flag_ref[steps * ROOM + slots * REACH + i] = jnp.where(i < count_ref[0], 1, 0)
    for s in reversed(range(steps)):
        k = s % 3
        base, before, after = 3 * ROOM * s, ROOM * s, ROOM * (s + 1)

        def step(d, found, k=k, base=base, before=before, after=after):
            for i in range(slots):
                q = slots * d + i
                need = flag_ref[after + q]
                sides = [near_ref[4 + i, 6 * d + 2 * k + j] for j in range(2)]
                list_ref[base + found] = q
                list_ref[base + ROOM + found] = sides[0]
                list_ref[base + 2 * ROOM + found] = sides[1]
                flag_ref[before + jnp.where(need > 0, q, total)] = 1
                for side in sides:
                    flag_ref[before + jnp.where((need > 0) & (side >= 0), side, total)] = 1
                found += need
            return found

        found = lax.fori_loop(s + 1, 2 * REACH - s, step, jnp.int32(0))
        for i in range(slots):
            for j in range(3):
                list_ref[base + ROOM * j + found + i] = total
        list_ref[3 * ROOM * steps + s] = found


def unpack(rows_here, chunk, per, narrow, x_ref, out_ref, lo_ref, hi_ref):
    block = 4 * per + 16
    cols = per * rows_here
    length = out_ref.shape[1]
    tiles = [
        unpacked([x_ref[pl.ds(n * block + q, per, stride=4), :] for q in range(4)], rows_here * chunk)
        for n in range(narrow)
    ]
    for r in range(2 * rows_here):
        for y in range(rows_here):
            pieces = [t[r][:, chunk * y : chunk * (y + 1)] for t in tiles]
            line = jnp.concatenate(pieces + [jnp.zeros((per, 2 * LANES - length), F32)], 1)
            lo_ref[pl.ds(r * cols + y, per, stride=rows_here), :] = line[:, :LANES]
            hi_ref[pl.ds(r * cols + y, per, stride=rows_here), :] = line[:, LANES:]
    out_ref[:, :LANES] = lo_ref[...]
    out_ref[:, LANES:] = hi_ref[:, : length - LANES]


def sweeps(
    slots, narrow, per, used, place_ref, count_ref, list_ref, recv_ref, before_ref, row_ref, after_ref,
    table_ref, out_ref, one_ref, two_ref, edge_ref, edge_smem, sem,
):
    block = 4 * per + 16
    low = jnp.zeros((8, LANES), F32)
    top = jnp.zeros((8, LANES), F32)
    for n in range(narrow):
        row = n * block + 4 * per
        low += recv_ref[row : row + 8, :]
        top += recv_ref[row + 8 : row + 16, :]
    edge_ref[0:8, :] = low
    edge_ref[8:16, :] = top
    copy = pltpu.make_async_copy(edge_ref, edge_smem, sem)
    copy.start()
    mine = place_ref[1]
    total = 2 * REACH + 1
    for r in range(total):
        at = mine + r + narrow - REACH
        place = (r - REACH + 4) % narrow

        @pl.when(at < narrow)
        def _(r=r, place=place):
            one_ref[slots * r : slots * (r + 1)] = before_ref[place]

        @pl.when((at >= narrow) & (at < 2 * narrow))
        def _(r=r, place=place):
            one_ref[slots * r : slots * (r + 1)] = row_ref[place]

        @pl.when(at >= 2 * narrow)
        def _(r=r, place=place):
            one_ref[slots * r : slots * (r + 1)] = after_ref[place]

    copy.wait()
    row = lax.broadcasted_iota(jnp.int32, (2 * EDGE, CELLS), 0)
    real = row < EDGE
    late_row = row % EDGE >= 8
    column = lax.broadcasted_iota(jnp.int32, (2 * EDGE, LANES), 1)
    real_half = real[:, :LANES]
    early_half = column < LANES // 2
    late_last = column % EDGE >= 8
    left = table_ref[4 * CELLS :, : 12 * EDGE]
    held = [one_ref, two_ref]
    for s in range(3 * SUBCYCLES):
        k = s % 3
        source, target = held[s % 2], held[1 - s % 2]
        base = 3 * ROOM * s
        rounds = (list_ref[3 * ROOM * 3 * SUBCYCLES + s] + slots - 1) // slots

        def ghost(e, q, side, part, is_real, k=k, base=base, source=source):
            near = list_ref[base + ROOM * (1 + side) + e]
            lane = q + slots * (mine - 1)
            face = 4 + 2 * k + side
            flat = jnp.where(is_real, edge_smem[face, lane], edge_smem[6 + face, lane])
            return jnp.where(near >= 0, source[jnp.maximum(near, 0), :, part], flat)

        if k == 0:

            def step(d, carry, base=base, source=source, target=target, ghost=ghost):
                every = slice(0, CELLS)
                for i in range(slots):
                    e = slots * d + i
                    q = list_ref[base + e]
                    around = jnp.where(late_row, ghost(e, q, 0, every, real), ghost(e, q, 1, every, real))
                    high, rest = split(jnp.concatenate([source[q], around], 0))
                    target[q] = mm(left, jnp.concatenate([high, rest, high], 0))
                return carry

        else:
            table = halves(table_ref, k - 1)

            def step(d, carry, k=k, base=base, source=source, target=target, ghost=ghost, table=table):
                lower, upper = slice(0, LANES), slice(LANES, CELLS)
                lines, goals = [], []
                for i in range(slots):
                    e = slots * d + i
                    q = list_ref[base + e]
                    goals.append(q)
                    near, far = source[q, :, lower], source[q, :, upper]
                    if k == 1:
                        before = ghost(e, q, 0, upper, real_half)
                        after = ghost(e, q, 1, lower, real_half)
                        sides = jnp.where(early_half, far, before), jnp.where(early_half, after, near)
                    else:
                        sides = [
                            jnp.where(late_last, ghost(e, q, 0, part, real_half), ghost(e, q, 1, part, real_half))
                            for part in (lower, upper)
                        ]
                    lines += [jnp.concatenate([near, sides[0]], 1), jnp.concatenate([far, sides[1]], 1)]
                done = mm3(split(jnp.concatenate(lines, 0)), table)
                for i, q in enumerate(goals):
                    for part, at in ((lower, 4 * EDGE * i), (upper, 4 * EDGE * i + 2 * EDGE)):
                        re, im = done[at : at + EDGE], done[at + EDGE : at + 2 * EDGE]
                        target[q, 0:EDGE, part] = re[:, :LANES] - im[:, LANES:]
                        target[q, EDGE:, part] = im[:, :LANES] + re[:, LANES:]
                return carry

        lax.fori_loop(0, rounds, step, 0)
    final = held[0]
    for i in range(slots):
        value = final[slots * REACH + i]
        out_ref[i] = jnp.where(i < count_ref[0], value, jnp.zeros_like(value))


def shifted(block, axis, distance):
    devices = range(lax.axis_size(axis))
    route = [((i - distance) % len(devices), i) for i in devices]
    return lax.ppermute(block, axis, route)


def call(kernel, outs, specs, scratch=(), params=PARAMS):
    return pl.pallas_call(
        kernel,
        out_shape=[jax.ShapeDtypeStruct(shape, dtype) for shape, dtype in outs],
        in_specs=specs,
        out_specs=[VMEM] * len(outs),
        scratch_shapes=list(scratch),
        compiler_params=params,
    )


def exchange(block, axis):
    parts = lax.axis_size(axis)
    shape = (parts, block.shape[0] // parts, block.shape[1])
    return lax.all_to_all(block.reshape(shape), axis, split_axis=0, concat_axis=0, tiled=True).reshape(block.shape)


def shards(base, fine_psi, counts, neighbors, base_cell):
    wide = lax.axis_size("wide")
    narrow = lax.axis_size("narrow")
    w_at = lax.axis_index("wide")
    n_at = lax.axis_index("narrow")
    _, rows_here, cols_here, length = base.shape
    slots = fine_psi.shape[0]
    chunk = length // narrow
    per = wide // narrow
    used = rows_here * chunk
    place = jnp.stack([w_at, n_at]).astype(jnp.int32)

    patches = fine_psi.reshape(1, slots, 2 * EDGE, CELLS)
    trio = jnp.concatenate([shifted(patches, "narrow", 1), patches, shifted(patches, "narrow", -1)], 0)
    row = jnp.concatenate([shifted(trio, "narrow", 3), trio, shifted(trio[:2], "narrow", -3)], 0)
    before = shifted(row, "wide", 1)
    after = shifted(row, "wide", -1)

    kr, ki = circulant(length)
    (sent,) = call(
        lambda *refs: along_last(rows_here, cols_here, narrow, *refs),
        [((narrow * (cols_here + 8), LANES), F32)],
        [pl.BlockSpec(memory_space=pl.ANY)] * 3,
        [
            pltpu.VMEM((2 * rows_here * cols_here, length), F32),
            pltpu.VMEM(neighbors.shape, jnp.int32),
            pltpu.VMEM((4 * length, length), BF16),
            pltpu.SemaphoreType.DMA((3,)),
        ],
        WHOLE,
    )(base.reshape(2 * rows_here * cols_here, length), neighbors, jnp.asarray(stacked(kr, ki)))
    first = exchange(sent, "narrow")

    full = np.stack([np.stack([kr, -ki]), np.stack([ki, kr])])
    second = full.transpose(0, 2, 1, 3).reshape(2, wide, rows_here, 2 * length).transpose(0, 2, 1, 3)
    second = stacked(second.reshape(2 * length, 2 * length))
    (sent,) = call(
        lambda *refs: along_second(rows_here, chunk, wide, narrow, *refs), [((wide * 4, LANES), F32)], [VMEM] * 2
    )(first, jnp.asarray(second))
    groups = base_cell.shape[0]
    cells = jnp.transpose(base_cell, (2, 1, 0)).reshape(18, groups)
    faces = groups // LANES * 8
    data, upto, count, hit, at, goal = call(
        lambda *refs: plan(rows_here, chunk, wide, *refs),
        [((faces, 5 * LANES), BF16), ((faces, LANES), F32), ((8, LANES), jnp.int32)]
        + [((LANES, LANES), F32), ((LANES, 2 * LANES), jnp.int32), ((8, LANES), jnp.int32)],
        [SMEM, VMEM],
    )(place, cells)

    got = exchange(sent, "wide")
    third = full.reshape(2, 2, wide, rows_here, wide, rows_here).transpose(0, 3, 2, 1, 5, 4)
    third = third.reshape(2 * length, 2 * rows_here, wide)
    main = third[:, :4].transpose(0, 2, 1).reshape(2 * length, 4 * wide)
    third = stacked(np.concatenate([main, third[:, 4:].reshape(2 * length, 2 * wide)], 1))
    (sent,) = call(
        lambda *refs: along_first(rows_here, chunk, wide, narrow, slots, *refs),
        [((wide * 16, LANES), F32)],
        [SMEM] + [VMEM] * 8,
        [pltpu.VMEM((16, groups + 2 * LANES), F32)],
    )(count, data, upto, hit, at, goal, first, got, jnp.asarray(third))
    got = exchange(sent, "wide")
    sent, near = call(
        lambda *refs: forward_rows(slots, wide, narrow, used, *refs),
        [((narrow * (4 * per + 16), LANES), F32), ((8, LANES), jnp.int32)],
        [SMEM, VMEM],
    )(place, got)
    got = exchange(sent, "narrow")
    (drifted,) = call(
        lambda *refs: unpack(rows_here, chunk, per, narrow, *refs),
        [((2 * rows_here * cols_here, length), F32)],
        [VMEM],
        [pltpu.VMEM((2 * rows_here * cols_here, LANES), F32)] * 2,
    )(got)

    total = 2 * REACH + 1
    entries = 3 * SUBCYCLES * 3 * ROOM + LANES
    lists = pl.pallas_call(
        lambda *refs: needs(slots, *refs),
        out_shape=jax.ShapeDtypeStruct((entries,), jnp.int32),
        in_specs=[SMEM] * 2,
        out_specs=SMEM,
        scratch_shapes=[pltpu.SMEM(((3 * SUBCYCLES + 1) * ROOM,), jnp.int32)],
        compiler_params=PARAMS,
    )(counts, near)
    (fine,) = call(
        lambda *refs: sweeps(slots, narrow, per, used, *refs),
        [((slots, 2 * EDGE, CELLS), F32)],
        [SMEM] * 3 + [VMEM] * 5,
        [
            pltpu.VMEM((total * slots + 1, 2 * EDGE, CELLS), F32),
            pltpu.VMEM((total * slots + 1, 2 * EDGE, CELLS), F32),
            pltpu.VMEM((16, LANES), F32),
            pltpu.SMEM((16, LANES), F32),
            pltpu.SemaphoreType.DMA,
        ],
    )(place, counts, lists, got, before, row, after, jnp.asarray(sweep_tables()))
    return (drifted.reshape(base.shape), fine.reshape(fine_psi.shape))


def solution(mesh):
    in_specs = (
        P(None, "wide", "narrow", None),
        P(("wide", "narrow"), None, None, None),
        P(("wide", "narrow")),
        P(("wide", "narrow"), None),
        P(),
    )
    out_specs = (P(None, "wide", "narrow", None), P(("wide", "narrow"), None, None, None))
    return jax.shard_map(shards, mesh=mesh, in_specs=in_specs, out_specs=out_specs, check_vma=False)
```
